128 devices in a mesh: row: 8 (over x, core), col: 16 (over y, z).
Axes of the slice: x: 4, y: 4, z: 4, core: 2. Of those that a mesh axis runs over, the one named last changes fastest.
Arguments:
- x_values: bfloat16 [16, 1048576], P(None, ('row', 'col')), may hold values from -6 to 6
- coords: float32 [3, 1048576], P(None, ('row', 'col')), may hold values from 0 to 1
- weights: float32 [1048576], P(('row', 'col')), may hold values from 0.005 to 0.05
- basis: bfloat16 [4096, 64, 256], P(('row', 'col')), may hold values from -0.375 to 0.375
- transfer: bfloat16 [512, 64, 512], P(('row', 'col')), may hold values from -0.25 to 0.25
- couple0: bfloat16 [4096, 64, 1728], P(('row', 'col')), may hold values from -0.15625 to 0.15625
- couple1: bfloat16 [512, 64, 1728], P(('row', 'col')), may hold values from -0.15625 to 0.15625
- first_far_partner_device: int32 [4096, 27], P(('row', 'col')), may hold values from 0 to 127, all different within a row; in each aligned block of 32 rows (0 to 31, 32 to 63, ...) at most 14 rows name the same one
- far0_box: int32 [4096, 27], P(('row', 'col')), may hold values from 0 to 31
- far1_dev: int32 [512, 27], P(('row', 'col')), may hold values from 0 to 127, all different within a row; in each aligned block of 4 rows (0 to 3, 4 to 7, ...) at most 2 rows name the same one
- far1_box: int32 [512, 27], P(('row', 'col')), may hold values from 0 to 3
- near_partner_device: int32 [4096, 8], P(('row', 'col')), may hold values from 0 to 127, all different within a row; in each aligned block of 32 rows (0 to 31, 32 to 63, ...) at most 4 rows name the same one
- near_box: int32 [4096, 8], P(('row', 'col')), may hold values from 0 to 31
Outputs:
- product: bfloat16 [16, 1048576], P(None, ('row', 'col'))
The draws below stay inside these ranges and needn't reach their ends.
Inputs may be any that keep to these rules, and one draw needn't show every extreme that they name: `first_far_partner_device`: each row names distinct devices. Among the rows of the leaf boxes of one device, no device is named more than 14 times, and in some device's rows some device is named exactly 14 times. `far1_dev`: each row names distinct devices. Among the rows of the parent boxes of one device, no device is named more than 2 times, and in some device's rows some device is named exactly 2 times. `near_partner_device`: each row names distinct devices. Among the rows of the leaf boxes of one device, no device is named more than 4 times, and in some device's rows some device is named exactly 4 times.
All inputs are finite; a program needn't handle non-finite values.
Results may differ from the reference program's by a relative error of at most 0.0051.
Values may be sent and summed in bfloat16 or wider, within the bound.
No kernel may reach another device: no remote copies, remote signals or barrier semaphores. Data moves between devices by JAX's collectives and lax.ppermute only.
A program may use at most 128 MiB of HBM per device.

```python
import math
import jax
import jax.numpy as jnp
import numpy as np
from jax import lax

LEAF = 256
K = 64
RHS = 16
BOX_DEV = 32
NFAR0 = 27
NFAR1 = 27
NNEAR = 8
PAR_DEV = 4
BOXES0 = 4096
BOXES1 = 512
POINTS = 1048576
CAP0 = 14
CAP1 = 2
CAPN = 4
N_ROW = 8
N_COL = 16


def set_ends(values, rng, smallest, largest):
    place = [jax.random.randint(jax.random.fold_in(rng, axis), (), 0, length) for axis, length in enumerate(values.shape)]
    widest = values.shape.index(max(values.shape))
    next_to = place[:widest] + [(place[widest] + 1) % values.shape[widest]] + place[widest + 1:]
    return values.at[tuple(place)].set(smallest).at[tuple(next_to)].set(largest)


def levels(key, shape, split, least, top_value):
    loudness = 1.0
    for dim, blocks in split:
        heights = jax.random.uniform(jax.random.fold_in(jax.random.fold_in(key, 6), dim), (blocks,), jnp.float32, least / len(split), top_value / len(split))
        loudness = loudness * jnp.repeat(jnp.exp(heights), shape[dim] // blocks).reshape((-1,) + (1,) * (len(shape) - 1 - dim))
    return loudness


def assign_block(key, own, number, rows, count, top, most, skew):
    ranking = jax.random.permutation(key, count)
    packed, common = load_shares(count, rows * top, most, skew, True), load_shares(count, rows * top, most, skew, False)
    places = jnp.arange(count)

    def named(lengths, offset_by):
        used = int((lengths > 0).sum())
        fixed = max(1, used // 4)
        passed = fixed + (places - fixed + offset_by * (used - fixed)) % max(1, count - fixed)
        return jnp.zeros((count,), jnp.int32).at[ranking[jnp.where(places < fixed, places, passed)]].set(jnp.asarray(lengths, jnp.int32))

    lengths = jnp.where(number % 4 == 0, named(packed, number // 4), named(common, number - number // 4 - 1))
    mixed = jax.random.permutation(jax.random.fold_in(own, 3), count)
    source_of, receiver = mixed[0:count // 2 * 2:2], mixed[1:count // 2 * 2:2]
    margin = jnp.minimum(lengths[source_of] - 1, most - lengths[receiver]) // 2
    margin = jnp.where((source_of == ranking[0]) | (receiver == ranking[0]) | (lengths[receiver] == 0), 0, jnp.maximum(margin, 0))
    passed = jax.random.randint(jax.random.fold_in(own, 4), (count // 2,), 0, 1 << 20) % (margin + 1)
    lengths = lengths.at[source_of].add(-passed).at[receiver].add(passed)
    members = jnp.searchsorted(jnp.cumsum(lengths), jnp.arange(rows * top), side="right").astype(jnp.int32)
    listing = members.reshape(top, rows).T
    listing = listing[jax.random.permutation(jax.random.fold_in(own, 1), rows)]
    offset_by = jax.random.randint(jax.random.fold_in(own, 2), (rows, 1), 0, top)
    return jnp.take_along_axis(listing, (jnp.arange(top)[None, :] + offset_by) % top, axis=1)


def load_shares(count, total, bound, skew, full):
    weights = [(1 << 20) // math.isqrt(rank ** skew) + 1 for rank in range(1, count + 1)]
    largest = bound if full else min(bound, max(-(-total // count), total * weights[0] // sum(weights)))
    least = 1 if total - largest >= count - 1 else 0
    holding, spare = [largest] + [least] * (count - 1), total - largest - least * (count - 1)
    while spare > 0:
        movable = [i for i in range(1, count) if holding[i] < largest] or [i for i in range(1, count) if holding[i] < bound]
        whole, budget = sum([weights[i] for i in movable]), spare
        for i in movable:
            more = min(bound - holding[i], max(1, budget * weights[i] // whole), spare)
            holding[i] = holding[i] + more
            spare = spare - more
    return np.array(holding)


def noise(stream_key, extent, deviation, limit, pieces=(), kind=jnp.bfloat16):
    loudness = levels(stream_key, extent, pieces, -0.22, 0.18) if pieces else 1.0
    entries = jax.random.normal(stream_key, extent, jnp.float32) * deviation * loudness
    return jnp.minimum(jnp.maximum(entries, -limit), limit).astype(kind)


def setup_inputs(seed: int = 0) -> dict:
    key_of = jax.random.split(jax.random.key(seed), 14)
    x_values = noise(key_of[0], (RHS, POINTS), 1.0, 6.0, ((1, 128),))
    coords = jnp.clip(1.0 * jax.random.uniform(key_of[1], (3, POINTS), jnp.float32) ** levels(key_of[1], (3, POINTS), ((1, 128),), -0.2, 0.2), 0.0, 1.0)
    weights = jnp.clip(jnp.exp(math.log(0.05) - 2.3025851 * jax.random.uniform(key_of[2], (POINTS,), jnp.float32) ** levels(key_of[2], (POINTS,), ((0, 128),), -0.2, 0.2)), 0.005, 0.05)
    basis = noise(key_of[3], (BOXES0, K, LEAF), LEAF ** -0.5, 0.375, ((0, 128),))
    transfer = noise(key_of[4], (BOXES1, K, 8 * K), (8 * K) ** -0.5, 0.25, ((0, 128),))
    couple0 = noise(key_of[5], (BOXES0, K, NFAR0 * K), (NFAR0 * K) ** -0.5, 0.15625, ((0, 128),))
    couple1 = noise(key_of[6], (BOXES1, K, NFAR1 * K), (NFAR1 * K) ** -0.5, 0.15625, ((0, 128),))
    first_far_partner_device_keys = jax.random.split(jax.random.fold_in(key_of[7], 1), BOXES0 // BOX_DEV)
    first_far_partner_device_turns = jax.random.permutation(jax.random.fold_in(key_of[7], 3), BOXES0 // BOX_DEV)
    first_far_partner_device = jax.vmap(lambda own, number: assign_block(jax.random.fold_in(key_of[7], 2), own, number, BOX_DEV, N_ROW * N_COL, NFAR0, CAP0, 2))(first_far_partner_device_keys, first_far_partner_device_turns).reshape((BOXES0, NFAR0))
    far0_box = set_ends(jax.random.randint(key_of[8], (BOXES0, NFAR0), 0, BOX_DEV), jax.random.fold_in(key_of[8], 1), 0, BOX_DEV - 1).astype(jnp.int32)
    far1_dev_keys = jax.random.split(jax.random.fold_in(key_of[9], 1), BOXES1 // PAR_DEV)
    far1_dev_turns = jax.random.permutation(jax.random.fold_in(key_of[9], 3), BOXES1 // PAR_DEV)
    far1_dev = jax.vmap(lambda own, number: assign_block(jax.random.fold_in(key_of[9], 2), own, number, PAR_DEV, N_ROW * N_COL, NFAR1, CAP1, 2))(far1_dev_keys, far1_dev_turns).reshape((BOXES1, NFAR1))
    far1_box = set_ends(jax.random.randint(key_of[10], (BOXES1, NFAR1), 0, PAR_DEV), jax.random.fold_in(key_of[10], 1), 0, PAR_DEV - 1).astype(jnp.int32)
    near_partner_device_keys = jax.random.split(jax.random.fold_in(key_of[11], 1), BOXES0 // BOX_DEV)
    near_partner_device_turns = jax.random.permutation(jax.random.fold_in(key_of[11], 3), BOXES0 // BOX_DEV)
    near_partner_device = jax.vmap(lambda own, number: assign_block(jax.random.fold_in(key_of[11], 2), own, number, BOX_DEV, N_ROW * N_COL, NNEAR, CAPN, 2))(near_partner_device_keys, near_partner_device_turns).reshape((BOXES0, NNEAR))
    near_box = set_ends(jax.random.randint(key_of[12], (BOXES0, NNEAR), 0, BOX_DEV), jax.random.fold_in(key_of[12], 1), 0, BOX_DEV - 1).astype(jnp.int32)
    return dict(x_values=x_values, coords=coords, weights=weights, basis=basis, transfer=transfer, couple0=couple0, couple1=couple1, first_far_partner_device=first_far_partner_device, far0_box=far0_box, far1_dev=far1_dev, far1_box=far1_box, near_partner_device=near_partner_device, near_box=near_box)


wave_number = 20.0
soften = 0.01

def kernel_block(targets, sources, value_entries):
    squared = jnp.zeros(targets.shape[:1] + sources.shape[1:2] + (targets.shape[2], sources.shape[3]), jnp.float32)
    for coordinate in range(3):
        offset = targets[:, None, coordinate, :, None] - sources[:, :, coordinate, None, :]
        squared = squared + offset * offset
    kernel_evaluator = jnp.cos(wave_number * jnp.sqrt(squared)) / jnp.sqrt(squared + soften) * sources[:, :, 3, None, :]
    kernel_evaluator = kernel_evaluator.astype(jnp.bfloat16)
    return jnp.einsum('qwoj,qwkj->qko', kernel_evaluator.astype(jnp.float32), value_entries.astype(jnp.float32))

def grouped(callable_routine, operands, group):
    total = operands[0].shape[0]
    folded = tuple((operand.reshape((total // group, group) + operand.shape[1:]) for operand in operands))
    result = lax.map(lambda member: callable_routine(*member), folded)
    return result.reshape((total,) + result.shape[2:])

def couple_level(coefficients, source_ids, matrices):
    listed = source_ids.shape[1]

    def one_group(identity, blocks):
        picked = coefficients[identity]
        stacked = picked.transpose(0, 2, 1, 3).reshape(picked.shape[0], RHS, listed * K)
        return jnp.einsum('brm,bkm->brk', stacked.astype(jnp.float32), blocks.astype(jnp.float32))
    return grouped(one_group, (source_ids, matrices), 64)

def reference(x_values, coords, weights, basis, transfer, couple0, couple1, first_far_partner_device, far0_box, far1_dev, far1_box, near_partner_device, near_box):
    columns = x_values.reshape(RHS, BOXES0, LEAF).transpose(1, 0, 2)
    leaf_coef = jnp.einsum('brl,bkl->brk', columns.astype(jnp.float32), basis.astype(jnp.float32)).astype(jnp.bfloat16)
    children = leaf_coef.reshape(BOXES1, 8, RHS, K).transpose(0, 2, 1, 3).reshape(BOXES1, RHS, 8 * K)
    parent_coef = jnp.einsum('prm,pkm->prk', children.astype(jnp.float32), transfer.astype(jnp.float32)).astype(jnp.bfloat16)
    leaf_ids = (first_far_partner_device * BOX_DEV + far0_box).astype(jnp.int32)
    parent_ids = (far1_dev * PAR_DEV + far1_box).astype(jnp.int32)
    leaf_far = couple_level(leaf_coef, leaf_ids, couple0)
    parent_far = couple_level(parent_coef, parent_ids, couple1)
    parent_down = parent_far.astype(jnp.bfloat16)
    spread_across = jnp.einsum('prk,pkm->prm', parent_down.astype(jnp.float32), transfer.astype(jnp.float32))
    spread_across = spread_across.reshape(BOXES1, RHS, 8, K).transpose(0, 2, 1, 3).reshape(BOXES0, RHS, K)
    field = (leaf_far + spread_across).astype(jnp.bfloat16)
    far_part = jnp.einsum('brk,bkl->brl', field.astype(jnp.float32), basis.astype(jnp.float32))
    geometry = jnp.concatenate([coords, weights[None, :]], 0).reshape(4, BOXES0, LEAF).transpose(1, 0, 2)
    own_ids = jnp.arange(BOXES0, dtype=jnp.int32)[:, None]
    near_ids = jnp.concatenate([own_ids, (near_partner_device * BOX_DEV + near_box).astype(jnp.int32)], 1)

    def near_group(identity, targets):
        return kernel_block(targets, geometry[identity], columns[identity])
    near_part = grouped(near_group, (near_ids, geometry[:, :3]), 64)
    total = (far_part + near_part).transpose(1, 0, 2).reshape(RHS, POINTS)
    return total.astype(jnp.bfloat16)
```

```python
import functools
import math

import jax
import jax.numpy as jnp
import numpy as np
from jax import lax
from jax.experimental import pallas as pl
from jax.experimental.pallas import tpu as pltpu
from jax.sharding import PartitionSpec as P

AXES = ("row", "col")
LEAF = 256
HALF = 128
WIDTH = 64
SIDES = 16
SLOTS = 4
PART = 2
ROWS = 40 * PART
FEATURES = 48
GROUP = 8
CODE = 248.0
CYCLES = 20.0 / (2.0 * math.pi)
SOFTEN = 0.01 * CYCLES * CYCLES
MAGIC = 12582912.0


def cosine_polynomial(degree):
    nodes = np.cos((np.arange(400) + 0.5) * np.pi / 400) * 0.125 + 0.125
    fit = np.polynomial.chebyshev.Chebyshev.interpolate(
        lambda z: np.cos(2 * np.pi * np.sqrt(np.maximum(z, 0.0))), degree, [0.0, 0.25]
    )
    del nodes
    return [float(c) for c in fit.convert(kind=np.polynomial.Polynomial).coef]


COSINE = cosine_polynomial(4)
LEAD = COSINE[-1]
MONIC = [c / LEAD for c in COSINE[:-1]]
FOLD = LEAD * CYCLES


def split(value):
    high = value.astype(jnp.bfloat16).astype(jnp.float32)
    low = (value - high).astype(jnp.bfloat16).astype(jnp.float32)
    return high, low


def contract_last(a, b):
    return lax.dot_general(a, b, (((1,), (1,)), ((), ())), preferred_element_type=jnp.float32)


def vmem():
    return pl.BlockSpec(memory_space=pltpu.VMEM)


def smem():
    return pl.BlockSpec(memory_space=pltpu.SMEM)


def coef_kernel(x_ref, basis_ref, transfer_ref, out_ref):
    boxes = basis_ref.shape[0]
    parents = transfer_ref.shape[0]
    leaf = []
    for b in range(boxes):
        c = contract_last(x_ref[:, b * LEAF : (b + 1) * LEAF], basis_ref[b])
        leaf.append(c)
        if b % 2:
            out_ref[b // 2] = jnp.concatenate([leaf[b - 1], c], axis=1).astype(jnp.bfloat16)
    up = []
    for p in range(parents):
        children = jnp.concatenate([out_ref[4 * p + i] for i in range(4)], axis=1)
        up.append(contract_last(children, transfer_ref[p]))
        if p % 2:
            out_ref[boxes // 2 + p // 2] = jnp.concatenate([up[p - 1], up[p]], axis=1).astype(
                jnp.bfloat16
            )


def plan_kernel(dev_ref, box_ref, asked_ref, place_ref):
    count, listed = dev_ref.shape
    devices = asked_ref.shape[0]
    lane = lax.broadcasted_iota(jnp.int32, (count, devices), 1)
    dev, box = dev_ref[...], box_ref[...]
    named = jnp.zeros((count, devices), jnp.float32)
    wanted = jnp.zeros((count, devices), jnp.float32)
    hits = []
    for i in range(listed):
        hit = (dev[:, i : i + 1] == lane).astype(jnp.float32)
        hits.append(hit)
        named = named + hit
        wanted = wanted + hit * box[:, i : i + 1].astype(jnp.float32)
    row = lax.broadcasted_iota(jnp.int32, (count, count), 0)
    col = lax.broadcasted_iota(jnp.int32, (count, count), 1)
    before = jnp.dot(
        (col < row).astype(jnp.bfloat16),
        named.astype(jnp.bfloat16),
        preferred_element_type=jnp.float32,
    )
    slot = lax.broadcasted_iota(jnp.int32, (devices, devices), 0)
    asked = jnp.zeros((devices, devices), jnp.float32)
    for p in range(SLOTS):
        here = jnp.sum(
            jnp.where((before == p) & (named > 0), wanted, 0.0), axis=0, keepdims=True
        )
        asked = jnp.where(slot == p, here, asked)
    asked_ref[...] = asked.T.astype(jnp.int32)
    column = lax.broadcasted_iota(jnp.int32, (count, listed), 1)
    position = jnp.zeros((count, listed), jnp.float32)
    for i in range(listed):
        at = jnp.sum(hits[i] * before, axis=1, keepdims=True)
        position = jnp.where(column == i, at, position)
    place_ref[...] = dev * SLOTS + position.astype(jnp.int32)


def prepare_kernel(x_ref, weight_ref, source_ref, target_ref, table_ref, feature_ref):
    boxes = target_ref.shape[0]
    for b in range(boxes):
        for h in range(2):
            at = b * LEAF + h * HALF
            values = x_ref[:, at : at + HALF].astype(jnp.float32)
            scaled = values * (weight_ref[0:1, at : at + HALF] * FOLD)
            first = (b % PART) * 32 + h * SIDES
            table_ref[b // PART, first : first + SIDES, :] = scaled.astype(jnp.bfloat16)
    for q in range(boxes // PART):
        table_ref[q, 32 * PART :, :] = jnp.exp2(CODE * (source_ref[q] - 0.5)).astype(jnp.bfloat16)

    sub = lax.broadcasted_iota(jnp.int32, (8, LEAF), 0)

    def one(b, carry):
        point = (target_ref[b] - 0.5) * CYCLES
        high, low = split(point)
        whole = high + low
        square = whole * whole
        norm = square[0:1] + square[1:2] + square[2:3]
        n1, rest = split(norm)
        n2, n3 = split(norm - n1)
        del rest
        last = jnp.where(sub == 0, n1, jnp.where(sub == 1, n2, jnp.where(sub == 2, n3, 0.0)))
        for h in range(2):
            here = (sub >= 4 * h) & (sub < 4 * h + 3)
            one_row = jnp.where(sub == 4 * h + 3, 1.0, 0.0)
            blocks = [
                jnp.where(here, -2.0 * high, one_row),
                jnp.where(here, -2.0 * low, one_row),
                jnp.where(here, -2.0 * high, one_row),
                jnp.where(here, -2.0 * low, 0.0),
                last,
                jnp.zeros_like(last),
            ]
            feature_ref[b, :, h * LEAF : (h + 1) * LEAF] = jnp.concatenate(blocks, 0).astype(
                jnp.bfloat16
            )
        return carry

    lax.fori_loop(0, boxes, one, 0)


def pack_kernel(asked_ref, table_ref, *out_refs):
    step = pl.program_id(0)
    block = out_refs[0].shape[0]

    def one(d, carry):
        for part, out_ref in enumerate(out_refs):
            coded = []
            for p in range(PART):
                q = asked_ref[step * block + d, part * PART + p]
                pair, side = q // PART, q % PART
                out_ref[d, 32 * p : 32 * (p + 1), :] = table_ref[
                    pair, pl.ds(pl.multiple_of(side * 32, 32), 32), :
                ]
                both = table_ref[pair, 32 * PART :, :].astype(jnp.float32)
                coded.append(jnp.where(side == 0, both[0:8], both[8:16]))
            out_ref[d, 32 * PART :, :] = jnp.concatenate(coded, 0).astype(jnp.bfloat16)
        return carry

    lax.fori_loop(0, block, one, 0)


def work_group(entry, source_ref, feature_ref, total_ref, square_ref, kernel_ref):
    sub = lax.broadcasted_iota(jnp.int32, (8, HALF), 0)
    norm_row = (sub % 4) == 3
    places = [entry(g) for g in range(GROUP)]
    for g, (target, place, side) in enumerate(places):
        both = source_ref[place, 32 * PART :, :].astype(jnp.float32)
        coded = jnp.where(side == 0, both[0:8], both[8:16])
        point = jnp.log2(coded) * (CYCLES / CODE)
        high, low = split(point)
        whole = high + low
        square = whole * whole
        norm = (
            pltpu.roll(square, 1, 0) + pltpu.roll(square, 2, 0) + pltpu.roll(square, 3, 0)
        )
        n1 = norm.astype(jnp.bfloat16).astype(jnp.float32)
        n2, n3 = split(norm - n1)
        ones = jnp.ones_like(norm)
        blocks = [
            jnp.where(norm_row, n1, high),
            jnp.where(norm_row, n2, high),
            jnp.where(norm_row, n3, low),
            low,
            ones,
            ones,
        ]
        features = jnp.concatenate(blocks, 0).T.astype(jnp.bfloat16)
        square_ref[g] = jnp.dot(
            features, feature_ref[target], preferred_element_type=jnp.float32
        )
    for g, (target, place, side) in enumerate(places):
        for h in range(2):
            for r in range(0, HALF, 32):
                d = jnp.maximum(square_ref[g, r : r + 32, h * LEAF : (h + 1) * LEAF], 1e-12)
                turns = d * lax.rsqrt(d)
                turns = turns - ((turns + MAGIC) - MAGIC)
                z = turns * turns
                value = z + MONIC[-1]
                for c in MONIC[-2::-1]:
                    value = value * z + c
                value = value * lax.rsqrt(d + SOFTEN)
                kernel_ref[g, h * HALF + r : h * HALF + r + 32, :] = value.astype(jnp.bfloat16)
        rows = source_ref[place, pl.ds(pl.multiple_of(side * 32, 32), 32), :]
        values = jnp.concatenate([rows[:SIDES], rows[SIDES:]], axis=1)
        total_ref[target] += jnp.dot(values, kernel_ref[g], preferred_element_type=jnp.float32)


def own_kernel(place_ref, table_ref, feature_ref, total_ref, list_ref, square_ref, kernel_ref):
    boxes, listed = place_ref.shape
    total_ref[...] = jnp.zeros_like(total_ref)

    def group(k, carry):
        def entry(g):
            b = k * GROUP + g
            return b, b // PART, b % PART

        work_group(entry, table_ref, feature_ref, total_ref, square_ref, kernel_ref)
        return carry

    lax.fori_loop(0, boxes // GROUP, group, 0)

    parts = list_ref.shape[0]

    def scan(b, counts):
        counts = list(counts)
        for i in range(listed):
            place = place_ref[b, i]
            part = (place % SLOTS) // PART
            code = b * 1024 + place
            for c in range(parts):
                list_ref[c, counts[c]] = code
                counts[c] = counts[c] + jnp.where(part == c, 1, 0)
        return tuple(counts)

    counts = lax.fori_loop(0, boxes, scan, (jnp.int32(0),) * parts)
    for c in range(parts):
        for k in range(GROUP):
            list_ref[c, counts[c] + k] = boxes * 1024
        list_ref[c, list_ref.shape[1] - 1] = (counts[c] + GROUP - 1) // GROUP


def near_kernel(part, list_ref, got_ref, feature_ref, old_ref, total_ref, square_ref, kernel_ref):
    total_ref[...] = old_ref[...]

    def group(k, carry):
        def entry(g):
            code = list_ref[part, k * GROUP + g]
            target, place = code // 1024, code % 1024
            return target, place // SLOTS, place % PART

        work_group(entry, got_ref, feature_ref, total_ref, square_ref, kernel_ref)
        return carry

    lax.fori_loop(0, list_ref[part, list_ref.shape[1] - 1], group, 0)


def far_kernel(
    dev0_ref, box0_ref, dev1_ref, box1_ref,
    table_ref, couple0_ref, couple1_ref, transfer_ref, basis_ref, near_ref, out_ref,
    stack_ref, up_ref,
):
    p = pl.program_id(0)
    listed = dev0_ref.shape[1]
    lane = lax.broadcasted_iota(jnp.int32, (SIDES, HALF), 1)
    share = table_ref.shape[0] // 128

    def piece(place, index, want):
        tile = table_ref[place].astype(jnp.float32)
        turn = jnp.where(index % 2 == want, 0, WIDTH)
        return pltpu.roll(tile, turn, 1)

    def gather(dev_ref, box_ref, row, first, into_ref, at):
        for j in range(0, listed, 2):
            parts = []
            for k in range(2):
                if j + k < listed:
                    index = box_ref[row, j + k]
                    parts.append(piece(dev_ref[row, j + k] * share + first + index // 2, index, k))
                else:
                    parts.append(jnp.zeros((SIDES, HALF), jnp.float32))
            into_ref[pl.ds(at, SIDES), j * WIDTH : (j + 2) * WIDTH] = jnp.where(
                lane < WIDTH, parts[0], parts[1]
            ).astype(jnp.bfloat16)

    def leaf(i, carry):
        gather(dev0_ref, box0_ref, 8 * p + i, 0, stack_ref, pl.multiple_of(i * SIDES, SIDES))
        return carry

    lax.fori_loop(0, 8, leaf, 0)
    gather(dev1_ref, box1_ref, p, 16, up_ref, 0)
    length = listed * WIDTH
    parent_far = contract_last(up_ref[:, :length], couple1_ref[0]).astype(jnp.bfloat16)
    down = jnp.dot(parent_far, transfer_ref[0], preferred_element_type=jnp.float32)
    for half in range(2):
        matrices = couple0_ref[4 * half : 4 * half + 4].reshape(4 * WIDTH, length)
        stacked = stack_ref[4 * half * SIDES : 4 * (half + 1) * SIDES, :length]
        product = contract_last(stacked, matrices)
        for k in range(4):
            i = 4 * half + k
            field = (
                product[k * SIDES : (k + 1) * SIDES, k * WIDTH : (k + 1) * WIDTH]
                + down[:, i * WIDTH : (i + 1) * WIDTH]
            ).astype(jnp.bfloat16)
            far = jnp.dot(field, basis_ref[i], preferred_element_type=jnp.float32)
            out_ref[:, i * LEAF : (i + 1) * LEAF] = (far + near_ref[i]).astype(jnp.bfloat16)


def on_device(
    x_values, coords, weights, basis, transfer, couple0, couple1,
    first_far_partner_device, far0_box, far1_dev, far1_box, near_partner_device, near_box,
):
    devices = lax.axis_size(AXES)
    boxes = basis.shape[0]
    parents = transfer.shape[0]
    listed = near_partner_device.shape[1]
    params = functools.partial(pltpu.CompilerParams, vmem_limit_bytes=48 * 2**20)
    rows = boxes // 2 + parents // 2

    coef = pl.pallas_call(
        coef_kernel,
        out_shape=jax.ShapeDtypeStruct((rows, SIDES, HALF), jnp.bfloat16),
        in_specs=[vmem()] * 3,
        out_specs=vmem(),
        compiler_params=params(),
        name="coef",
    )(x_values, basis, transfer)
    table = lax.all_gather(coef, AXES, axis=0, tiled=True)

    asked, place = pl.pallas_call(
        plan_kernel,
        out_shape=(
            jax.ShapeDtypeStruct((devices, devices), jnp.int32),
            jax.ShapeDtypeStruct((boxes, listed), jnp.int32),
        ),
        in_specs=[vmem()] * 2,
        out_specs=(vmem(), vmem()),
        compiler_params=params(),
        name="plan",
    )(near_partner_device, near_box)
    requests = lax.all_to_all(
        asked.reshape(devices, 1, devices), AXES, split_axis=0, concat_axis=0, tiled=True
    ).reshape(devices, devices)

    halves = coords.reshape(3, boxes, 2, HALF).transpose(1, 2, 0, 3)
    source = jnp.pad(halves, ((0, 0), (0, 0), (0, 1), (0, 0)), constant_values=0.5)
    source = source.reshape(boxes // PART, 8 * PART, HALF)
    target = jnp.pad(coords.reshape(3, boxes, LEAF), ((0, 1), (0, 0), (0, 0)), constant_values=0.5)
    target = target.transpose(1, 0, 2)
    target = jnp.concatenate([target, target], axis=1)
    own, features = pl.pallas_call(
        prepare_kernel,
        out_shape=(
            jax.ShapeDtypeStruct((boxes // PART, ROWS, HALF), jnp.bfloat16),
            jax.ShapeDtypeStruct((boxes + 1, FEATURES, 2 * LEAF), jnp.bfloat16),
        ),
        in_specs=[vmem()] * 4,
        out_specs=(vmem(), vmem()),
        compiler_params=params(),
        name="prepare",
    )(x_values, weights.reshape(1, boxes * LEAF), source, target)

    scratch = [
        pltpu.VMEM((GROUP, HALF, 2 * LEAF), jnp.float32),
        pltpu.VMEM((GROUP, LEAF, LEAF), jnp.bfloat16),
    ]
    parts = SLOTS // PART
    pairs = boxes * LEAF * LEAF
    total_shape = jax.ShapeDtypeStruct((boxes + 1, SIDES, LEAF), jnp.float32)
    near, listing = pl.pallas_call(
        own_kernel,
        out_shape=(total_shape, jax.ShapeDtypeStruct((parts, 384), jnp.int32)),
        in_specs=[smem(), vmem(), vmem()],
        out_specs=(vmem(), smem()),
        scratch_shapes=scratch,
        compiler_params=params(),
        cost_estimate=pl.CostEstimate(
            flops=40 * pairs, bytes_accessed=4 << 20, transcendentals=2 * pairs
        ),
        name="own",
    )(place, own, features)

    per_step = 16
    packed = pl.pallas_call(
        pack_kernel,
        out_shape=[jax.ShapeDtypeStruct((devices, ROWS, HALF), jnp.bfloat16)] * parts,
        grid=(devices // per_step,),
        in_specs=[smem(), pl.BlockSpec((boxes // PART, ROWS, HALF), lambda i: (0, 0, 0))],
        out_specs=[pl.BlockSpec((per_step, ROWS, HALF), lambda i: (i, 0, 0))] * parts,
        compiler_params=params(),
        name="pack",
    )(requests, own)

    for part in range(parts):
        got = lax.all_to_all(packed[part], AXES, split_axis=0, concat_axis=0, tiled=True)
        near = pl.pallas_call(
            functools.partial(near_kernel, part),
            out_shape=total_shape,
            in_specs=[smem(), vmem(), vmem(), vmem()],
            out_specs=vmem(),
            scratch_shapes=scratch,
            input_output_aliases={3: 0},
            compiler_params=params(),
            cost_estimate=pl.CostEstimate(
                flops=160 * pairs, bytes_accessed=8 << 20, transcendentals=8 * pairs
            ),
            name="near",
        )(listing, got, features, near)

    length = couple0.shape[2]
    padded = (length + HALF - 1) // HALF * HALF
    return pl.pallas_call(
        far_kernel,
        out_shape=jax.ShapeDtypeStruct((SIDES, boxes * LEAF), jnp.bfloat16),
        grid=(parents,),
        in_specs=[
            smem(), smem(), smem(), smem(),
            pl.BlockSpec((devices * rows, SIDES, HALF), lambda i: (0, 0, 0)),
            pl.BlockSpec((8, WIDTH, length), lambda i: (i, 0, 0)),
            pl.BlockSpec((1, WIDTH, length), lambda i: (i, 0, 0)),
            pl.BlockSpec((1, WIDTH, 8 * WIDTH), lambda i: (i, 0, 0)),
            pl.BlockSpec((8, WIDTH, LEAF), lambda i: (i, 0, 0)),
            pl.BlockSpec((8, SIDES, LEAF), lambda i: (i, 0, 0)),
        ],
        out_specs=pl.BlockSpec((SIDES, 8 * LEAF), lambda i: (0, i)),
        scratch_shapes=[
            pltpu.VMEM((8 * SIDES, padded), jnp.bfloat16),
            pltpu.VMEM((SIDES, padded), jnp.bfloat16),
        ],
        compiler_params=params(),
        name="far",
    )(
        first_far_partner_device, far0_box, far1_dev, far1_box,
        table, couple0, couple1, transfer, basis, near,
    )


def solution(mesh):
    placed = (
        P(None, AXES),
        P(None, AXES),
        P(AXES),
        P(AXES, None, None),
        P(AXES, None, None),
        P(AXES, None, None),
        P(AXES, None, None),
        P(AXES, None),
        P(AXES, None),
        P(AXES, None),
        P(AXES, None),
        P(AXES, None),
        P(AXES, None),
    )
    return jax.shard_map(
        on_device, mesh=mesh, in_specs=placed, out_specs=P(None, AXES), check_vma=False
    )
```

```python
import functools
import math

import jax
import jax.numpy as jnp
import numpy as np
from jax import lax
from jax.experimental import pallas as pl
from jax.experimental.pallas import tpu as pltpu
from jax.sharding import PartitionSpec as P

AXES = ("row", "col")
LEAF = 256
HALF = 128
WIDTH = 64
SIDES = 16
SLOTS = 4
PART = 2
ROWS = 40 * PART
FEATURES = 48
GROUP = 8
BIAS = 1e-5
CODE = 248.0
CYCLES = 20.0 / (2.0 * math.pi)
SOFTEN = 0.01 * CYCLES * CYCLES


def cosine_polynomial(degree):
    fit = np.polynomial.chebyshev.Chebyshev.interpolate(
        lambda z: np.cos(2 * np.pi * np.sqrt(np.maximum(z, 0.0))), degree, [0.0, 0.25]
    )
    return [float(c) for c in fit.convert(kind=np.polynomial.Polynomial).coef]


COSINE = cosine_polynomial(4)
LEAD = COSINE[-1]
MONIC = [c / LEAD for c in COSINE[:-1]]
FOLD = LEAD * CYCLES


def split(value):
    high = value.astype(jnp.bfloat16).astype(jnp.float32)
    low = (value - high).astype(jnp.bfloat16).astype(jnp.float32)
    return high, low


def contract_last(a, b):
    return lax.dot_general(a, b, (((1,), (1,)), ((), ())), preferred_element_type=jnp.float32)


def vmem():
    return pl.BlockSpec(memory_space=pltpu.VMEM)


def smem():
    return pl.BlockSpec(memory_space=pltpu.SMEM)


def coef_kernel(x_ref, basis_ref, transfer_ref, out_ref):
    boxes = basis_ref.shape[0]
    parents = transfer_ref.shape[0]
    leaf = []
    for b in range(boxes):
        c = contract_last(x_ref[:, b * LEAF : (b + 1) * LEAF], basis_ref[b])
        leaf.append(c)
        if b % 2:
            out_ref[b // 2] = jnp.concatenate([leaf[b - 1], c], axis=1).astype(jnp.bfloat16)
    up = []
    for p in range(parents):
        children = jnp.concatenate([out_ref[4 * p + i] for i in range(4)], axis=1)
        up.append(contract_last(children, transfer_ref[p]))
        if p % 2:
            out_ref[boxes // 2 + p // 2] = jnp.concatenate([up[p - 1], up[p]], axis=1).astype(
                jnp.bfloat16
            )


def plan_kernel(dev_ref, box_ref, asked_ref, place_ref):
    listed, count = dev_ref.shape
    devices = asked_ref.shape[0]
    owner = lax.broadcasted_iota(jnp.int32, (devices, count), 0)
    dev, box = dev_ref[...], box_ref[...]
    named = jnp.zeros((devices, count), jnp.float32)
    wanted = jnp.zeros((devices, count), jnp.float32)
    hits = []
    for i in range(listed):
        hit = (dev[i : i + 1] == owner).astype(jnp.float32)
        hits.append(hit)
        named = named + hit
        wanted = wanted + hit * box[i : i + 1].astype(jnp.float32)
    row = lax.broadcasted_iota(jnp.int32, (count, count), 0)
    col = lax.broadcasted_iota(jnp.int32, (count, count), 1)
    before = jnp.dot(
        named.astype(jnp.bfloat16),
        (row < col).astype(jnp.bfloat16),
        preferred_element_type=jnp.float32,
    )
    slot = lax.broadcasted_iota(jnp.int32, (devices, devices), 1)
    asked = jnp.zeros((devices, devices), jnp.float32)
    for p in range(SLOTS):
        here = jnp.sum(
            jnp.where((before == p) & (named > 0), wanted, 0.0), axis=1, keepdims=True
        )
        asked = jnp.where(slot == p, here, asked)
    asked_ref[...] = asked.astype(jnp.int32)
    position = [jnp.sum(hit * before, axis=0, keepdims=True) for hit in hits]
    place_ref[...] = dev * SLOTS + jnp.concatenate(position, axis=0).astype(jnp.int32)


def prepare_kernel(
    x_ref, weight_ref, source_ref, target_ref, table_ref, coded_ref, feature_ref
):
    boxes = target_ref.shape[0]
    for b in range(boxes):
        for h in range(2):
            at = b * LEAF + h * HALF
            values = x_ref[:, at : at + HALF].astype(jnp.float32)
            scaled = values * (weight_ref[0:1, at : at + HALF] * FOLD)
            first = (b % PART) * 32 + h * SIDES
            table_ref[b // PART, first : first + SIDES, :] = scaled.astype(jnp.bfloat16)
    for q in range(boxes // PART):
        coded = jnp.exp2(CODE * (source_ref[q] - 0.5)).astype(jnp.bfloat16)
        table_ref[q, 32 * PART :, :] = coded
        for p in range(PART):
            coded_ref[PART * q + p] = coded.astype(jnp.float32)[8 * p : 8 * (p + 1)]

    sub = lax.broadcasted_iota(jnp.int32, (8, LEAF), 0)

    def one(b, carry):
        point = (target_ref[b] - 0.5) * CYCLES
        high, low = split(point)
        whole = high + low
        square = whole * whole
        norm = square[0:1] + square[1:2] + square[2:3] + BIAS
        n1 = norm.astype(jnp.bfloat16).astype(jnp.float32)
        n2, n3 = split(norm - n1)
        last = jnp.where(sub == 0, n1, jnp.where(sub == 1, n2, jnp.where(sub == 2, n3, 0.0)))
        for h in range(2):
            here = (sub >= 4 * h) & (sub < 4 * h + 3)
            one_row = jnp.where(sub == 4 * h + 3, 1.0, 0.0)
            blocks = [
                jnp.where(here, -2.0 * high, one_row),
                jnp.where(here, -2.0 * low, one_row),
                jnp.where(here, -2.0 * high, one_row),
                jnp.where(here, -2.0 * low, 0.0),
                last,
                jnp.zeros_like(last),
            ]
            feature_ref[b, :, h * LEAF : (h + 1) * LEAF] = jnp.concatenate(blocks, 0).astype(
                jnp.bfloat16
            )
        return carry

    lax.fori_loop(0, boxes, one, 0)


def pack_kernel(asked_ref, table_ref, coded_ref, *out_refs):
    step = pl.program_id(0)
    block = out_refs[0].shape[0]

    def one(k, carry):
        for d in (2 * k, 2 * k + 1):
            for part, out_ref in enumerate(out_refs):
                coded = []
                for p in range(PART):
                    q = asked_ref[step * block + d, part * PART + p]
                    side = pl.multiple_of(q % PART * 32, 32)
                    out_ref[d, 32 * p : 32 * (p + 1), :] = table_ref[q // PART, pl.ds(side, 32), :]
                    coded.append(coded_ref[q])
                out_ref[d, 32 * PART :, :] = jnp.concatenate(coded, 0).astype(jnp.bfloat16)
        return carry

    lax.fori_loop(0, block // 2, one, 0)


def start_pair(entry, source_ref, feature_ref, square_ref, g):
    target, place, side = entry
    sub = lax.broadcasted_iota(jnp.int32, (8, HALF), 0)
    norm_row = (sub % 4) == 3
    both = source_ref[place, 32 * PART :, :].astype(jnp.float32)
    coded = jnp.where(side == 0, both[0:8], both[8:16])
    point = jnp.log2(coded) * (CYCLES / CODE)
    high, low = split(point)
    whole = high + low
    square = whole * whole
    norm = pltpu.roll(square, 1, 0) + pltpu.roll(square, 2, 0) + pltpu.roll(square, 3, 0)
    n1 = norm.astype(jnp.bfloat16).astype(jnp.float32)
    n2, n3 = split(norm - n1)
    ones = jnp.ones_like(norm)
    blocks = [
        jnp.where(norm_row, n1, high),
        jnp.where(norm_row, n2, high),
        jnp.where(norm_row, n3, low),
        low,
        ones,
        ones,
    ]
    features = jnp.concatenate(blocks, 0).T.astype(jnp.bfloat16)
    square_ref[g] = jnp.dot(features, feature_ref[target], preferred_element_type=jnp.float32)


def values_of_pair(square_ref, kernel_ref, g):
    for h in range(2):
        for r in range(0, HALF, 32):
            d = square_ref[g, r : r + 32, h * LEAF : (h + 1) * LEAF]
            turns = d * lax.rsqrt(d)
            turns = turns - jnp.round(turns)
            z = turns * turns
            value = z + MONIC[-1]
            for c in MONIC[-2::-1]:
                value = value * z + c
            value = value * lax.rsqrt(d + SOFTEN)
            kernel_ref[g, h * HALF + r : h * HALF + r + 32, :] = value.astype(jnp.bfloat16)


def finish_pair(entry, source_ref, total_ref, kernel_ref, g):
    target, place, side = entry
    rows = source_ref[place, pl.ds(pl.multiple_of(side * 32, 32), 32), :]
    values = jnp.concatenate([rows[:SIDES], rows[SIDES:]], axis=1)
    total_ref[target] += jnp.dot(values, kernel_ref[g], preferred_element_type=jnp.float32)


def work(groups, entry, source_ref, feature_ref, total_ref, square_ref, kernel_ref):
    for g in range(GROUP):
        start_pair(entry(g), source_ref, feature_ref, square_ref, g)

    def body(k, carry):
        for half in range(2):
            at = (2 * k + half) * GROUP
            mine = half * GROUP
            for g in range(GROUP):
                start_pair(
                    entry(at + GROUP + g), source_ref, feature_ref, square_ref, GROUP - mine + g
                )
                values_of_pair(square_ref, kernel_ref, mine + g)
                if g:
                    finish_pair(entry(at + g - 1), source_ref, total_ref, kernel_ref, mine + g - 1)
            finish_pair(entry(at + GROUP - 1), source_ref, total_ref, kernel_ref, mine + GROUP - 1)
        return carry

    lax.fori_loop(0, groups, body, 0)


def own_kernel(place_ref, table_ref, feature_ref, total_ref, list_ref, square_ref, kernel_ref):
    listed, boxes = place_ref.shape
    total_ref[...] = jnp.zeros_like(total_ref)

    def entry(k):
        b = jnp.minimum(k, boxes - 1)
        return b, b // PART, b % PART

    groups = boxes // (2 * GROUP)
    work(groups, entry, table_ref, feature_ref, total_ref, square_ref, kernel_ref)

    parts = list_ref.shape[0]

    def scan(b, counts):
        counts = list(counts)
        for i in range(listed):
            place = place_ref[i, b]
            part = (place % SLOTS) // PART
            code = b * 1024 + place
            for c in range(parts):
                list_ref[c, counts[c]] = code
                counts[c] = counts[c] + jnp.where(part == c, 1, 0)
        return tuple(counts)

    counts = lax.fori_loop(0, boxes, scan, (jnp.int32(0),) * parts)
    for c in range(parts):
        for k in range(3 * GROUP):
            list_ref[c, counts[c] + k] = boxes * 1024
        list_ref[c, list_ref.shape[1] - 1] = (counts[c] + 2 * GROUP - 1) // (2 * GROUP)


def near_kernel(part, list_ref, got_ref, feature_ref, old_ref, total_ref, square_ref, kernel_ref):
    total_ref[...] = old_ref[...]

    def entry(k):
        code = list_ref[part, k]
        target, place = code // 1024, code % 1024
        return target, place // SLOTS, place % PART

    groups = list_ref[part, list_ref.shape[1] - 1]
    work(groups, entry, got_ref, feature_ref, total_ref, square_ref, kernel_ref)


def far_kernel(
    code0_ref, code1_ref, table_ref, couple0_ref, couple1_ref, transfer_ref, basis_ref, near_ref,
    out_ref, stack_ref, up_ref,
):
    listed = code0_ref.shape[1]
    length = listed * WIDTH
    lane = lax.broadcasted_iota(jnp.int32, (SIDES, HALF), 1)

    def piece(code_ref, row, j):
        code = code_ref[row, j]
        tile = table_ref[code // 2]
        return jnp.where((code + j) % 2 == 0, tile, pltpu.roll(tile, WIDTH, 1))

    def gather(code_ref, row, into_ref, at):
        for j in range(0, listed, 2):
            tile = piece(code_ref, row, j)
            if j + 1 < listed:
                tile = jnp.where(lane < WIDTH, tile, piece(code_ref, row, j + 1))
            into_ref[pl.ds(at, SIDES), j * WIDTH : (j + 2) * WIDTH] = tile

    def parent(p, carry):
        gather(code1_ref, p, up_ref, 0)
        for i in range(8):
            gather(code0_ref, 8 * p + i, stack_ref, i * SIDES)
        parent_far = contract_last(up_ref[:, :length], couple1_ref[p]).astype(jnp.bfloat16)
        down = jnp.dot(parent_far, transfer_ref[p], preferred_element_type=jnp.float32)
        for half in range(2):
            first = 8 * p + 4 * half
            matrices = couple0_ref[pl.ds(first, 4)].reshape(4 * WIDTH, length)
            stacked = stack_ref[4 * half * SIDES : 4 * (half + 1) * SIDES, :length]
            product = contract_last(stacked, matrices)
            for k in range(4):
                i = 4 * half + k
                field = (
                    product[k * SIDES : (k + 1) * SIDES, k * WIDTH : (k + 1) * WIDTH]
                    + down[:, i * WIDTH : (i + 1) * WIDTH]
                ).astype(jnp.bfloat16)
                far = jnp.dot(field, basis_ref[first + k], preferred_element_type=jnp.float32)
                at = pl.multiple_of((first + k) * LEAF, LEAF)
                out_ref[:, pl.ds(at, LEAF)] = (far + near_ref[first + k]).astype(jnp.bfloat16)
        return carry

    lax.fori_loop(0, transfer_ref.shape[0], parent, 0)


def on_device(
    x_values, coords, weights, basis, transfer, couple0, couple1,
    first_far_partner_device, far0_box, far1_dev, far1_box, near_partner_device, near_box,
):
    devices = lax.axis_size(AXES)
    boxes = basis.shape[0]
    parents = transfer.shape[0]
    listed = near_partner_device.shape[1]

    def params(mib):
        return pltpu.CompilerParams(vmem_limit_bytes=mib * 2**20)

    rows = boxes // 2 + parents // 2

    coef = pl.pallas_call(
        coef_kernel,
        out_shape=jax.ShapeDtypeStruct((rows, SIDES, HALF), jnp.bfloat16),
        in_specs=[vmem()] * 3,
        out_specs=vmem(),
        compiler_params=params(8),
        name="coef",
    )(x_values, basis, transfer)
    table = lax.all_gather(coef, AXES, axis=0, tiled=True)

    asked, place = pl.pallas_call(
        plan_kernel,
        out_shape=(
            jax.ShapeDtypeStruct((devices, devices), jnp.int32),
            jax.ShapeDtypeStruct((listed, boxes), jnp.int32),
        ),
        in_specs=[vmem()] * 2,
        out_specs=(vmem(), vmem()),
        compiler_params=params(8),
        name="plan",
    )(near_partner_device.T, near_box.T)
    requests = lax.all_to_all(
        asked.reshape(devices, 1, devices), AXES, split_axis=0, concat_axis=0, tiled=True
    ).reshape(devices, devices)

    halves = coords.reshape(3, boxes, 2, HALF).transpose(1, 2, 0, 3)
    source = jnp.pad(halves, ((0, 0), (0, 0), (0, 1), (0, 0)), constant_values=0.5)
    source = source.reshape(boxes // PART, 8 * PART, HALF)
    target = jnp.pad(coords.reshape(3, boxes, LEAF), ((0, 1), (0, 0), (0, 0)), constant_values=0.5)
    target = target.transpose(1, 0, 2)
    target = jnp.concatenate([target, target], axis=1)
    own, coded, features = pl.pallas_call(
        prepare_kernel,
        out_shape=(
            jax.ShapeDtypeStruct((boxes // PART, ROWS, HALF), jnp.bfloat16),
            jax.ShapeDtypeStruct((boxes, 8, HALF), jnp.float32),
            jax.ShapeDtypeStruct((boxes + 1, FEATURES, 2 * LEAF), jnp.bfloat16),
        ),
        in_specs=[vmem()] * 4,
        out_specs=(vmem(), vmem(), vmem()),
        compiler_params=params(8),
        name="prepare",
    )(x_values, weights.reshape(1, boxes * LEAF), source, target)

    scratch = [
        pltpu.VMEM((2 * GROUP, HALF, 2 * LEAF), jnp.float32),
        pltpu.VMEM((2 * GROUP, LEAF, LEAF), jnp.bfloat16),
    ]
    parts = SLOTS // PART
    pairs = boxes * LEAF * LEAF
    per_step = 16
    packed = pl.pallas_call(
        pack_kernel,
        out_shape=[jax.ShapeDtypeStruct((devices, ROWS, HALF), jnp.bfloat16)] * parts,
        grid=(devices // per_step,),
        in_specs=[
            smem(),
            pl.BlockSpec((boxes // PART, ROWS, HALF), lambda i: (0, 0, 0)),
            pl.BlockSpec((boxes, 8, HALF), lambda i: (0, 0, 0)),
        ],
        out_specs=[pl.BlockSpec((per_step, ROWS, HALF), lambda i: (i, 0, 0))] * parts,
        compiler_params=params(8),
        name="pack",
    )(requests, own, coded)

    packed, own, features = lax.optimization_barrier((packed, own, features))
    total_shape = jax.ShapeDtypeStruct((boxes + 1, SIDES, LEAF), jnp.float32)
    near, listing = pl.pallas_call(
        own_kernel,
        out_shape=(total_shape, jax.ShapeDtypeStruct((parts, 384), jnp.int32)),
        in_specs=[smem(), vmem(), vmem()],
        out_specs=(vmem(), smem()),
        scratch_shapes=scratch,
        compiler_params=params(12),
        cost_estimate=pl.CostEstimate(
            flops=40 * pairs, bytes_accessed=4 << 20, transcendentals=2 * pairs
        ),
        name="own",
    )(place, own, features)
    later, near, listing = lax.optimization_barrier((packed[1:], near, listing))
    packed = [packed[0], *later]

    for part in range(parts):
        got = lax.all_to_all(packed[part], AXES, split_axis=0, concat_axis=0, tiled=True)
        near = pl.pallas_call(
            functools.partial(near_kernel, part),
            out_shape=total_shape,
            in_specs=[smem(), vmem(), vmem(), vmem()],
            out_specs=vmem(),
            scratch_shapes=scratch,
            input_output_aliases={3: 0},
            compiler_params=params(12),
            cost_estimate=pl.CostEstimate(
                flops=160 * pairs, bytes_accessed=8 << 20, transcendentals=8 * pairs
            ),
            name="near",
        )(listing, got, features, near)

    padded = (couple0.shape[2] + HALF - 1) // HALF * HALF
    return pl.pallas_call(
        far_kernel,
        out_shape=jax.ShapeDtypeStruct((SIDES, boxes * LEAF), jnp.bfloat16),
        in_specs=[smem(), smem()] + [vmem()] * 6,
        out_specs=vmem(),
        scratch_shapes=[
            pltpu.VMEM((8 * SIDES, padded), jnp.bfloat16),
            pltpu.VMEM((SIDES, padded), jnp.bfloat16),
        ],
        compiler_params=params(8),
        name="far",
    )(
        first_far_partner_device * (2 * rows) + far0_box,
        far1_dev * (2 * rows) + boxes + far1_box,
        table, couple0, couple1, transfer, basis, near,
    )


def solution(mesh):
    placed = (
        P(None, AXES),
        P(None, AXES),
        P(AXES),
        P(AXES, None, None),
        P(AXES, None, None),
        P(AXES, None, None),
        P(AXES, None, None),
        P(AXES, None),
        P(AXES, None),
        P(AXES, None),
        P(AXES, None),
        P(AXES, None),
        P(AXES, None),
    )
    return jax.shard_map(
        on_device, mesh=mesh, in_specs=placed, out_specs=P(None, AXES), check_vma=False
    )
```

```python
import functools
import math

import jax
import jax.numpy as jnp
import numpy as np
from jax import lax
from jax.experimental import pallas as pl
from jax.experimental.pallas import tpu as pltpu
from jax.sharding import PartitionSpec as P

AXES = ("row", "col")
LEAF = 256
HALF = 128
WIDTH = 64
SIDES = 16
SLOTS = 4
PART = 2
ROWS = 40 * PART
FEATURES = 48
GROUP = 8
BIAS = 1e-5
CODE = 248.0
CYCLES = 20.0 / (2.0 * math.pi)
SOFTEN = 0.01 * CYCLES * CYCLES


def cosine_polynomial(degree):
    fit = np.polynomial.chebyshev.Chebyshev.interpolate(
        lambda z: np.cos(2 * np.pi * np.sqrt(np.maximum(z, 0.0))), degree, [0.0, 0.25]
    )
    return [float(c) for c in fit.convert(kind=np.polynomial.Polynomial).coef]


COSINE = cosine_polynomial(4)
LEAD = COSINE[-1]
MONIC = [c / LEAD for c in COSINE[:-1]]
FOLD = LEAD * CYCLES


def split(value):
    high = value.astype(jnp.bfloat16).astype(jnp.float32)
    low = (value - high).astype(jnp.bfloat16).astype(jnp.float32)
    return high, low


def shifted(number, by):
    return lax.shift_right_logical(number, jnp.int32(by.bit_length() - 1))


def contract_last(a, b):
    return lax.dot_general(a, b, (((1,), (1,)), ((), ())), preferred_element_type=jnp.float32)


def vmem():
    return pl.BlockSpec(memory_space=pltpu.VMEM)


def hbm():
    return pl.BlockSpec(memory_space=pltpu.HBM)


def smem():
    return pl.BlockSpec(memory_space=pltpu.SMEM)


def plan(dev_ref, box_ref, asked_ref, place_ref):
    listed, count = dev_ref.shape
    devices = asked_ref.shape[0]
    owner = lax.broadcasted_iota(jnp.int32, (devices, count), 0)
    dev, box = dev_ref[...], box_ref[...]
    named = jnp.zeros((devices, count), jnp.float32)
    wanted = jnp.zeros((devices, count), jnp.float32)
    hits = []
    for i in range(listed):
        hit = (dev[i : i + 1] == owner).astype(jnp.float32)
        hits.append(hit)
        named = named + hit
        wanted = wanted + hit * box[i : i + 1].astype(jnp.float32)
    row = lax.broadcasted_iota(jnp.int32, (count, count), 0)
    col = lax.broadcasted_iota(jnp.int32, (count, count), 1)
    before = jnp.dot(
        named.astype(jnp.bfloat16),
        (row < col).astype(jnp.bfloat16),
        preferred_element_type=jnp.float32,
    )
    slot = lax.broadcasted_iota(jnp.int32, (devices, devices), 1)
    asked = jnp.zeros((devices, devices), jnp.float32)
    for p in range(SLOTS):
        here = jnp.sum(
            jnp.where((before == p) & (named > 0), wanted, 0.0), axis=1, keepdims=True
        )
        asked = jnp.where(slot == p, here, asked)
    asked_ref[...] = asked.astype(jnp.int32)
    position = [jnp.sum(hit * before, axis=0, keepdims=True) for hit in hits]
    place_ref[...] = dev * SLOTS + jnp.concatenate(position, axis=0).astype(jnp.int32)


def coefficients(x_ref, basis_ref, transfer_ref, out_ref, arrived):
    boxes = basis_ref.shape[0]
    parents = transfer_ref.shape[0]
    leaf, up = [], []
    for b in range(boxes):
        if b % 8 == 0:
            arrived(b // 8)
        leaf.append(contract_last(x_ref[:, b * LEAF : (b + 1) * LEAF], basis_ref[b]))
        if b % 2:
            out_ref[b // 2] = jnp.concatenate(leaf[b - 1 :], axis=1).astype(jnp.bfloat16)
    for p in range(parents):
        children = jnp.concatenate([out_ref[4 * p + i] for i in range(4)], axis=1)
        up.append(contract_last(children, transfer_ref[p]))
        if p % 2:
            out_ref[boxes // 2 + p // 2] = jnp.concatenate(up[p - 1 :], axis=1).astype(jnp.bfloat16)


def first_kernel(
    x_hbm, basis_hbm, transfer_hbm, dev_hbm, box_hbm, coef_ref, asked_ref, place_ref,
    x_ref, basis_ref, transfer_ref, dev_ref, box_ref, sems,
):
    lists = [
        pltpu.make_async_copy(dev_hbm, dev_ref, sems.at[0]),
        pltpu.make_async_copy(box_hbm, box_ref, sems.at[1]),
    ]
    arrays = [
        pltpu.make_async_copy(x_hbm, x_ref, sems.at[2]),
        pltpu.make_async_copy(transfer_hbm, transfer_ref, sems.at[3]),
    ]
    eights = [
        pltpu.make_async_copy(
            basis_hbm.at[8 * i : 8 * i + 8], basis_ref.at[8 * i : 8 * i + 8], sems.at[4 + i]
        )
        for i in range(basis_ref.shape[0] // 8)
    ]
    for copy in lists + arrays + eights:
        copy.start()
    for copy in lists:
        copy.wait()
    plan(dev_ref, box_ref, asked_ref, place_ref)
    for copy in arrays:
        copy.wait()
    coefficients(x_ref, basis_ref, transfer_ref, coef_ref, lambda i: eights[i].wait())


def prepare_kernel(
    x_ref, weight_ref, source_ref, target_ref, table_ref, coded_ref, feature_ref
):
    boxes = target_ref.shape[0]
    for b in range(boxes):
        for h in range(2):
            at = b * LEAF + h * HALF
            values = x_ref[:, at : at + HALF].astype(jnp.float32)
            scaled = values * (weight_ref[0:1, at : at + HALF] * FOLD)
            first = (b % PART) * 32 + h * SIDES
            table_ref[b // PART, first : first + SIDES, :] = scaled.astype(jnp.bfloat16)
    for q in range(boxes // PART):
        coded = jnp.exp2(CODE * (source_ref[q] - 0.5)).astype(jnp.bfloat16)
        table_ref[q, 32 * PART :, :] = coded
        for p in range(PART):
            coded_ref[PART * q + p] = coded.astype(jnp.float32)[8 * p : 8 * (p + 1)]

    sub = lax.broadcasted_iota(jnp.int32, (8, LEAF), 0)

    def one(b, carry):
        point = (target_ref[b] - 0.5) * CYCLES
        high, low = split(point)
        whole = high + low
        square = whole * whole
        norm = square[0:1] + square[1:2] + square[2:3] + BIAS
        n1 = norm.astype(jnp.bfloat16).astype(jnp.float32)
        n2, n3 = split(norm - n1)
        last = jnp.where(sub == 0, n1, jnp.where(sub == 1, n2, jnp.where(sub == 2, n3, 0.0)))
        for h in range(2):
            here = (sub >= 4 * h) & (sub < 4 * h + 3)
            one_row = jnp.where(sub == 4 * h + 3, 1.0, 0.0)
            blocks = [
                jnp.where(here, -2.0 * high, one_row),
                jnp.where(here, -2.0 * low, one_row),
                jnp.where(here, -2.0 * high, one_row),
                jnp.where(here, -2.0 * low, 0.0),
                last,
                jnp.zeros_like(last),
            ]
            feature_ref[b, :, h * LEAF : (h + 1) * LEAF] = jnp.concatenate(blocks, 0).astype(
                jnp.bfloat16
            )
        return carry

    lax.fori_loop(0, boxes, one, 0)


def pack_kernel(asked_ref, table_ref, coded_ref, *out_refs):
    step = pl.program_id(0)
    block = out_refs[0].shape[0]

    def one(k, carry):
        for d in [4 * k + i for i in range(4)]:
            for part, out_ref in enumerate(out_refs):
                coded = []
                for p in range(PART):
                    q = asked_ref[step * block + d, part * PART + p]
                    side = pl.multiple_of((q & (PART - 1)) * 32, 32)
                    out_ref[d, 32 * p : 32 * (p + 1), :] = table_ref[
                        shifted(q, PART), pl.ds(side, 32), :
                    ]
                    coded.append(coded_ref[q])
                out_ref[d, 32 * PART :, :] = jnp.concatenate(coded, 0).astype(jnp.bfloat16)
        return carry

    lax.fori_loop(0, block // 4, one, 0)


def start_pair(entry, source_ref, feature_ref, square_ref, g):
    target, place, side = entry
    sub = lax.broadcasted_iota(jnp.int32, (8, HALF), 0)
    norm_row = (sub % 4) == 3
    both = source_ref[place, 32 * PART :, :].astype(jnp.float32)
    coded = jnp.where(side == 0, both[0:8], both[8:16])
    point = jnp.log2(coded) * (CYCLES / CODE)
    high, low = split(point)
    whole = high + low
    square = whole * whole
    norm = pltpu.roll(square, 1, 0) + pltpu.roll(square, 2, 0) + pltpu.roll(square, 3, 0)
    n1 = norm.astype(jnp.bfloat16).astype(jnp.float32)
    n2, n3 = split(norm - n1)
    ones = jnp.ones_like(norm)
    blocks = [
        jnp.where(norm_row, n1, high),
        jnp.where(norm_row, n2, high),
        jnp.where(norm_row, n3, low),
        low,
        ones,
        ones,
    ]
    features = jnp.concatenate(blocks, 0).T.astype(jnp.bfloat16)
    square_ref[g] = jnp.dot(features, feature_ref[target], preferred_element_type=jnp.float32)


def values_of_pair(square_ref, kernel_ref, g):
    for h in range(2):
        for r in range(0, HALF, 32):
            d = square_ref[g, r : r + 32, h * LEAF : (h + 1) * LEAF]
            turns = d * lax.rsqrt(d)
            turns = turns - jnp.round(turns)
            z = turns * turns
            value = z + MONIC[-1]
            for c in MONIC[-2::-1]:
                value = value * z + c
            value = value * lax.rsqrt(d + SOFTEN)
            kernel_ref[g, h * HALF + r : h * HALF + r + 32, :] = value.astype(jnp.bfloat16)


def finish_pair(entry, source_ref, total_ref, kernel_ref, g):
    target, place, side = entry
    rows = source_ref[place, pl.ds(pl.multiple_of(side * 32, 32), 32), :]
    values = jnp.concatenate([rows[:SIDES], rows[SIDES:]], axis=1)
    total_ref[target] += jnp.dot(values, kernel_ref[g], preferred_element_type=jnp.float32)


def work(groups, entry, source_ref, feature_ref, total_ref, square_ref, kernel_ref):
    for g in range(GROUP):
        start_pair(entry(g), source_ref, feature_ref, square_ref, g)

    def body(k, carry):
        for half in range(2):
            at = (2 * k + half) * GROUP
            mine = half * GROUP
            for g in range(GROUP):
                start_pair(
                    entry(at + GROUP + g), source_ref, feature_ref, square_ref, GROUP - mine + g
                )
                values_of_pair(square_ref, kernel_ref, mine + g)
                if g:
                    finish_pair(entry(at + g - 1), source_ref, total_ref, kernel_ref, mine + g - 1)
            finish_pair(entry(at + GROUP - 1), source_ref, total_ref, kernel_ref, mine + GROUP - 1)
        return carry

    lax.fori_loop(0, groups, body, 0)


def own_kernel(place_ref, table_ref, feature_ref, total_ref, list_ref, square_ref, kernel_ref):
    listed, boxes = place_ref.shape
    total_ref[...] = jnp.zeros_like(total_ref)

    def entry(k):
        b = jnp.minimum(k, boxes - 1)
        return b, shifted(b, PART), b & (PART - 1)

    groups = boxes // (2 * GROUP)
    work(groups, entry, table_ref, feature_ref, total_ref, square_ref, kernel_ref)

    parts = list_ref.shape[0]

    def scan(b, counts):
        counts = list(counts)
        for i in range(listed):
            place = place_ref[i, b]
            part = shifted(place & (SLOTS - 1), PART)
            code = b * 1024 + place
            for c in range(parts):
                list_ref[c, counts[c]] = code
                counts[c] = counts[c] + jnp.where(part == c, 1, 0)
        return tuple(counts)

    counts = lax.fori_loop(0, boxes, scan, (jnp.int32(0),) * parts)
    for c in range(parts):
        for k in range(3 * GROUP):
            list_ref[c, counts[c] + k] = boxes * 1024
        list_ref[c, list_ref.shape[1] - 1] = (counts[c] + 2 * GROUP - 1) // (2 * GROUP)


def near_kernel(part, list_ref, got_ref, feature_ref, old_ref, total_ref, square_ref, kernel_ref):
    total_ref[...] = old_ref[...]

    def entry(k):
        code = list_ref[part, k]
        return shifted(code, 1024), shifted(code & 1023, SLOTS), code & (PART - 1)

    groups = list_ref[part, list_ref.shape[1] - 1]
    work(groups, entry, got_ref, feature_ref, total_ref, square_ref, kernel_ref)


def far_kernel(
    code0_ref, code1_ref, table_hbm, couple0_hbm, couple1_ref, transfer_ref, basis_ref, near_ref,
    out_ref, table_ref, couple0_ref, stack_ref, up_ref, sems,
):
    listed = code0_ref.shape[1]
    parents = transfer_ref.shape[0]
    length = listed * WIDTH
    lane = lax.broadcasted_iota(jnp.int32, (SIDES, HALF), 1)
    size = table_ref.shape[0] // 4
    quarters = [
        pltpu.make_async_copy(
            table_hbm.at[i * size : (i + 1) * size],
            table_ref.at[i * size : (i + 1) * size],
            sems.at[i],
        )
        for i in range(4)
    ]
    eights = [
        pltpu.make_async_copy(
            couple0_hbm.at[8 * p : 8 * p + 8], couple0_ref.at[8 * p : 8 * p + 8], sems.at[4 + p]
        )
        for p in range(parents)
    ]
    for copy in quarters + eights:
        copy.start()
    for copy in quarters:
        copy.wait()

    def piece(code_ref, row, j):
        code = code_ref[row, j]
        tile = table_ref[shifted(code, 2)]
        return jnp.where(((code + j) & 1) == 0, tile, pltpu.roll(tile, WIDTH, 1))

    def gather(code_ref, row, into_ref, at):
        for j in range(0, listed, 2):
            tile = piece(code_ref, row, j)
            if j + 1 < listed:
                tile = jnp.where(lane < WIDTH, tile, piece(code_ref, row, j + 1))
            into_ref[at : at + SIDES, j * WIDTH : (j + 2) * WIDTH] = tile

    def gather_parent(p):
        gather(code1_ref, p, up_ref.at[p % 2], 0)
        for i in range(8):
            gather(code0_ref, 8 * p + i, stack_ref.at[p % 2], i * SIDES)

    gather_parent(0)
    for p in range(parents):
        eights[p].wait()
        if p + 1 < parents:
            gather_parent(p + 1)
        parent_far = contract_last(up_ref[p % 2, :, :length], couple1_ref[p]).astype(jnp.bfloat16)
        down = jnp.dot(parent_far, transfer_ref[p], preferred_element_type=jnp.float32)
        for half in range(2):
            first = 8 * p + 4 * half
            matrices = couple0_ref[first : first + 4].reshape(4 * WIDTH, length)
            stacked = stack_ref[p % 2, 4 * half * SIDES : 4 * (half + 1) * SIDES, :length]
            product = contract_last(stacked, matrices)
            for k in range(4):
                i = 4 * half + k
                field = (
                    product[k * SIDES : (k + 1) * SIDES, k * WIDTH : (k + 1) * WIDTH]
                    + down[:, i * WIDTH : (i + 1) * WIDTH]
                ).astype(jnp.bfloat16)
                far = jnp.dot(field, basis_ref[first + k], preferred_element_type=jnp.float32)
                at = (first + k) * LEAF
                out_ref[:, at : at + LEAF] = (far + near_ref[first + k]).astype(jnp.bfloat16)


def on_device(
    x_values, coords, weights, basis, transfer, couple0, couple1,
    first_far_partner_device, far0_box, far1_dev, far1_box, near_partner_device, near_box,
):
    devices = lax.axis_size(AXES)
    boxes = basis.shape[0]
    parents = transfer.shape[0]
    listed = near_partner_device.shape[1]

    def params(mib):
        return pltpu.CompilerParams(vmem_limit_bytes=mib * 2**20)

    rows = boxes // 2 + parents // 2

    coef, asked, place = pl.pallas_call(
        first_kernel,
        out_shape=(
            jax.ShapeDtypeStruct((rows, SIDES, HALF), jnp.bfloat16),
            jax.ShapeDtypeStruct((devices, devices), jnp.int32),
            jax.ShapeDtypeStruct((listed, boxes), jnp.int32),
        ),
        in_specs=[hbm()] * 5,
        out_specs=(vmem(), vmem(), vmem()),
        scratch_shapes=[
            pltpu.VMEM(x_values.shape, jnp.bfloat16),
            pltpu.VMEM(basis.shape, jnp.bfloat16),
            pltpu.VMEM(transfer.shape, jnp.bfloat16),
            pltpu.VMEM((listed, boxes), jnp.int32),
            pltpu.VMEM((listed, boxes), jnp.int32),
            pltpu.SemaphoreType.DMA((4 + boxes // 8,)),
        ],
        compiler_params=params(60),
        name="first",
    )(x_values, basis, transfer, near_partner_device.T, near_box.T)
    table = lax.all_gather(coef, AXES, axis=0, tiled=True)
    requests = lax.all_to_all(
        asked.reshape(devices, 1, devices), AXES, split_axis=0, concat_axis=0, tiled=True
    ).reshape(devices, devices)

    halves = coords.reshape(3, boxes, 2, HALF).transpose(1, 2, 0, 3)
    source = jnp.pad(halves, ((0, 0), (0, 0), (0, 1), (0, 0)), constant_values=0.5)
    source = source.reshape(boxes // PART, 8 * PART, HALF)
    target = jnp.pad(coords.reshape(3, boxes, LEAF), ((0, 1), (0, 0), (0, 0)), constant_values=0.5)
    target = target.transpose(1, 0, 2)
    target = jnp.concatenate([target, target], axis=1)
    own, coded, features = pl.pallas_call(
        prepare_kernel,
        out_shape=(
            jax.ShapeDtypeStruct((boxes // PART, ROWS, HALF), jnp.bfloat16),
            jax.ShapeDtypeStruct((boxes, 8, HALF), jnp.float32),
            jax.ShapeDtypeStruct((boxes + 1, FEATURES, 2 * LEAF), jnp.bfloat16),
        ),
        in_specs=[vmem()] * 4,
        out_specs=(vmem(), vmem(), vmem()),
        compiler_params=params(8),
        name="prepare",
    )(x_values, weights.reshape(1, boxes * LEAF), source, target)

    scratch = [
        pltpu.VMEM((2 * GROUP, HALF, 2 * LEAF), jnp.float32),
        pltpu.VMEM((2 * GROUP, LEAF, LEAF), jnp.bfloat16),
    ]
    parts = SLOTS // PART
    pairs = boxes * LEAF * LEAF
    per_step = 16
    packed = pl.pallas_call(
        pack_kernel,
        out_shape=[jax.ShapeDtypeStruct((devices, ROWS, HALF), jnp.bfloat16)] * parts,
        grid=(devices // per_step,),
        in_specs=[
            smem(),
            pl.BlockSpec((boxes // PART, ROWS, HALF), lambda i: (0, 0, 0)),
            pl.BlockSpec((boxes, 8, HALF), lambda i: (0, 0, 0)),
        ],
        out_specs=[pl.BlockSpec((per_step, ROWS, HALF), lambda i: (i, 0, 0))] * parts,
        compiler_params=params(59),
        name="pack",
    )(requests, own, coded)

    packed, own, features = lax.optimization_barrier((packed, own, features))
    total_shape = jax.ShapeDtypeStruct((boxes + 1, SIDES, LEAF), jnp.float32)
    near, listing = pl.pallas_call(
        own_kernel,
        out_shape=(total_shape, jax.ShapeDtypeStruct((parts, 384), jnp.int32)),
        in_specs=[smem(), vmem(), vmem()],
        out_specs=(vmem(), smem()),
        scratch_shapes=scratch,
        compiler_params=params(12),
        cost_estimate=pl.CostEstimate(
            flops=40 * pairs, bytes_accessed=4 << 20, transcendentals=2 * pairs
        ),
        name="own",
    )(place, own, features)
    later, near, listing = lax.optimization_barrier((packed[1:], near, listing))
    packed = [packed[0], *later]

    for part in range(parts):
        got = lax.all_to_all(packed[part], AXES, split_axis=0, concat_axis=0, tiled=True)
        near = pl.pallas_call(
            functools.partial(near_kernel, part),
            out_shape=total_shape,
            in_specs=[smem(), vmem(), vmem(), vmem()],
            out_specs=vmem(),
            scratch_shapes=scratch,
            input_output_aliases={3: 0},
            compiler_params=params(12),
            cost_estimate=pl.CostEstimate(
                flops=160 * pairs, bytes_accessed=8 << 20, transcendentals=8 * pairs
            ),
            name="near",
        )(listing, got, features, near)

    padded = (couple0.shape[2] + HALF - 1) // HALF * HALF
    return pl.pallas_call(
        far_kernel,
        out_shape=jax.ShapeDtypeStruct((SIDES, boxes * LEAF), jnp.bfloat16),
        in_specs=[smem(), smem(), hbm(), hbm()] + [vmem()] * 4,
        out_specs=vmem(),
        scratch_shapes=[
            pltpu.VMEM(table.shape, jnp.bfloat16),
            pltpu.VMEM(couple0.shape, jnp.bfloat16),
            pltpu.VMEM((2, 8 * SIDES, padded), jnp.bfloat16),
            pltpu.VMEM((2, SIDES, padded), jnp.bfloat16),
            pltpu.SemaphoreType.DMA((4 + parents,)),
        ],
        compiler_params=params(56),
        name="far",
    )(
        first_far_partner_device * (2 * rows) + far0_box,
        far1_dev * (2 * rows) + boxes + far1_box,
        table, couple0, couple1, transfer, basis, near,
    )


def solution(mesh):
    placed = (
        P(None, AXES),
        P(None, AXES),
        P(AXES),
        P(AXES, None, None),
        P(AXES, None, None),
        P(AXES, None, None),
        P(AXES, None, None),
        P(AXES, None),
        P(AXES, None),
        P(AXES, None),
        P(AXES, None),
        P(AXES, None),
        P(AXES, None),
    )
    return jax.shard_map(
        on_device, mesh=mesh, in_specs=placed, out_specs=P(None, AXES), check_vma=False
    )
```

```python
import functools
import math

import jax
import jax.numpy as jnp
import numpy as np
from jax import lax
from jax.experimental import pallas as pl
from jax.experimental.pallas import tpu as pltpu
from jax.sharding import PartitionSpec as P

AXES = ("row", "col")
LEAF = 256
HALF = 128
WIDTH = 64
SIDES = 16
SLOTS = 4
PART = 2
ROWS = 40 * PART
FEATURES = 48
GROUP = 8
BIAS = 1e-5
CODE = 248.0
CYCLES = 20.0 / (2.0 * math.pi)
SOFTEN = 0.01 * CYCLES * CYCLES


def cosine_polynomial(degree):
    fit = np.polynomial.chebyshev.Chebyshev.interpolate(
        lambda z: np.cos(2 * np.pi * np.sqrt(np.maximum(z, 0.0))), degree, [0.0, 0.25]
    )
    return [float(c) for c in fit.convert(kind=np.polynomial.Polynomial).coef]


COSINE = cosine_polynomial(4)
LEAD = COSINE[-1]
MONIC = [c / LEAD for c in COSINE[:-1]]
FOLD = LEAD * CYCLES


def split(value):
    high = value.astype(jnp.bfloat16).astype(jnp.float32)
    low = (value - high).astype(jnp.bfloat16).astype(jnp.float32)
    return high, low


def shifted(number, by):
    return lax.shift_right_logical(number, jnp.int32(by.bit_length() - 1))


def contract_last(a, b):
    return lax.dot_general(a, b, (((1,), (1,)), ((), ())), preferred_element_type=jnp.float32)


def vmem():
    return pl.BlockSpec(memory_space=pltpu.VMEM)


def hbm():
    return pl.BlockSpec(memory_space=pltpu.HBM)


def smem():
    return pl.BlockSpec(memory_space=pltpu.SMEM)


def plan(dev_ref, box_ref, asked_ref, place_ref):
    listed, count = dev_ref.shape
    devices = asked_ref.shape[0]
    owner = lax.broadcasted_iota(jnp.int32, (devices, count), 0)
    dev, box = dev_ref[...], box_ref[...]
    named = jnp.zeros((devices, count), jnp.float32)
    wanted = jnp.zeros((devices, count), jnp.float32)
    hits = []
    for i in range(listed):
        hit = (dev[i : i + 1] == owner).astype(jnp.float32)
        hits.append(hit)
        named = named + hit
        wanted = wanted + hit * box[i : i + 1].astype(jnp.float32)
    row = lax.broadcasted_iota(jnp.int32, (count, count), 0)
    col = lax.broadcasted_iota(jnp.int32, (count, count), 1)
    before = jnp.dot(
        named.astype(jnp.bfloat16),
        (row < col).astype(jnp.bfloat16),
        preferred_element_type=jnp.float32,
    )
    slot = lax.broadcasted_iota(jnp.int32, (devices, devices), 1)
    asked = jnp.zeros((devices, devices), jnp.float32)
    for p in range(SLOTS):
        here = jnp.sum(
            jnp.where((before == p) & (named > 0), wanted, 0.0), axis=1, keepdims=True
        )
        asked = jnp.where(slot == p, here, asked)
    asked_ref[...] = asked.astype(jnp.int32)
    position = [jnp.sum(hit * before, axis=0, keepdims=True) for hit in hits]
    place_ref[...] = dev * SLOTS + jnp.concatenate(position, axis=0).astype(jnp.int32)


def coefficients(x_ref, basis_ref, transfer_ref, out_ref, arrived):
    boxes = basis_ref.shape[0]
    parents = transfer_ref.shape[0]
    leaf, up = [], []
    for b in range(boxes):
        if b % 8 == 0:
            arrived(b // 8)
        leaf.append(contract_last(x_ref[:, b * LEAF : (b + 1) * LEAF], basis_ref[b]))
        if b % 2:
            out_ref[b // 2] = jnp.concatenate(leaf[b - 1 :], axis=1).astype(jnp.bfloat16)
    for p in range(parents):
        children = jnp.concatenate([out_ref[4 * p + i] for i in range(4)], axis=1)
        up.append(contract_last(children, transfer_ref[p]))
        if p % 2:
            out_ref[boxes // 2 + p // 2] = jnp.concatenate(up[p - 1 :], axis=1).astype(jnp.bfloat16)


def first_kernel(
    x_hbm, basis_hbm, transfer_hbm, dev_hbm, box_hbm, coef_ref, asked_ref, place_ref,
    x_ref, basis_ref, transfer_ref, dev_ref, box_ref, sems,
):
    lists = [
        pltpu.make_async_copy(dev_hbm, dev_ref, sems.at[0]),
        pltpu.make_async_copy(box_hbm, box_ref, sems.at[1]),
    ]
    arrays = [
        pltpu.make_async_copy(x_hbm, x_ref, sems.at[2]),
        pltpu.make_async_copy(transfer_hbm, transfer_ref, sems.at[3]),
    ]
    eights = [
        pltpu.make_async_copy(
            basis_hbm.at[8 * i : 8 * i + 8], basis_ref.at[8 * i : 8 * i + 8], sems.at[4 + i]
        )
        for i in range(basis_ref.shape[0] // 8)
    ]
    for copy in lists + arrays + eights:
        copy.start()
    for copy in lists:
        copy.wait()
    plan(dev_ref, box_ref, asked_ref, place_ref)
    for copy in arrays:
        copy.wait()
    coefficients(x_ref, basis_ref, transfer_ref, coef_ref, lambda i: eights[i].wait())


def prepare_kernel(
    x_ref, weight_ref, source_ref, target_ref, table_ref, coded_ref, feature_ref
):
    boxes = target_ref.shape[0]
    for b in range(boxes):
        for h in range(2):
            at = b * LEAF + h * HALF
            values = x_ref[:, at : at + HALF].astype(jnp.float32)
            scaled = values * (weight_ref[0:1, at : at + HALF] * FOLD)
            first = (b % PART) * 32 + h * SIDES
            table_ref[b // PART, first : first + SIDES, :] = scaled.astype(jnp.bfloat16)
    for q in range(boxes // PART):
        coded = jnp.exp2(CODE * (source_ref[q] - 0.5)).astype(jnp.bfloat16)
        table_ref[q, 32 * PART :, :] = coded
        for p in range(PART):
            coded_ref[PART * q + p] = coded.astype(jnp.float32)[8 * p : 8 * (p + 1)]

    sub = lax.broadcasted_iota(jnp.int32, (8, LEAF), 0)

    def one(b, carry):
        point = (target_ref[b] - 0.5) * CYCLES
        high, low = split(point)
        whole = high + low
        square = whole * whole
        norm = square[0:1] + square[1:2] + square[2:3] + BIAS
        n1 = norm.astype(jnp.bfloat16).astype(jnp.float32)
        n2, n3 = split(norm - n1)
        last = jnp.where(sub == 0, n1, jnp.where(sub == 1, n2, jnp.where(sub == 2, n3, 0.0)))
        for h in range(2):
            here = (sub >= 4 * h) & (sub < 4 * h + 3)
            one_row = jnp.where(sub == 4 * h + 3, 1.0, 0.0)
            blocks = [
                jnp.where(here, -2.0 * high, one_row),
                jnp.where(here, -2.0 * low, one_row),
                jnp.where(here, -2.0 * high, one_row),
                jnp.where(here, -2.0 * low, 0.0),
                last,
                jnp.zeros_like(last),
            ]
            feature_ref[b, :, h * LEAF : (h + 1) * LEAF] = jnp.concatenate(blocks, 0).astype(
                jnp.bfloat16
            )
        return carry

    lax.fori_loop(0, boxes, one, 0)


def pack_kernel(part, asked_ref, table_ref, coded_ref, out_ref):
    step = pl.program_id(0)
    block = out_ref.shape[0]

    def one(k, carry):
        for d in [4 * k + i for i in range(4)]:
            coded = []
            for p in range(PART):
                q = asked_ref[step * block + d, part * PART + p]
                side = pl.multiple_of((q & (PART - 1)) * 32, 32)
                out_ref[d, 32 * p : 32 * (p + 1), :] = table_ref[
                    shifted(q, PART), pl.ds(side, 32), :
                ]
                coded.append(coded_ref[q])
            out_ref[d, 32 * PART :, :] = jnp.concatenate(coded, 0).astype(jnp.bfloat16)
        return carry

    lax.fori_loop(0, block // 4, one, 0)


def start_pair(entry, source_ref, feature_ref, square_ref, g):
    target, place, side = entry
    sub = lax.broadcasted_iota(jnp.int32, (8, HALF), 0)
    norm_row = (sub % 4) == 3
    both = source_ref[place, 32 * PART :, :].astype(jnp.float32)
    coded = jnp.where(side == 0, both[0:8], both[8:16])
    point = jnp.log2(coded) * (CYCLES / CODE)
    high, low = split(point)
    whole = high + low
    square = whole * whole
    norm = pltpu.roll(square, 1, 0) + pltpu.roll(square, 2, 0) + pltpu.roll(square, 3, 0)
    n1 = norm.astype(jnp.bfloat16).astype(jnp.float32)
    n2, n3 = split(norm - n1)
    ones = jnp.ones_like(norm)
    blocks = [
        jnp.where(norm_row, n1, high),
        jnp.where(norm_row, n2, high),
        jnp.where(norm_row, n3, low),
        low,
        ones,
        ones,
    ]
    features = jnp.concatenate(blocks, 0).T.astype(jnp.bfloat16)
    square_ref[g] = jnp.dot(features, feature_ref[target], preferred_element_type=jnp.float32)


def values_of_pair(square_ref, kernel_ref, g):
    for h in range(2):
        for r in range(0, HALF, 32):
            d = square_ref[g, r : r + 32, h * LEAF : (h + 1) * LEAF]
            turns = d * lax.rsqrt(d)
            turns = turns - jnp.round(turns)
            z = turns * turns
            value = z + MONIC[-1]
            for c in MONIC[-2::-1]:
                value = value * z + c
            value = value * lax.rsqrt(d + SOFTEN)
            kernel_ref[g, h * HALF + r : h * HALF + r + 32, :] = value.astype(jnp.bfloat16)


def finish_pair(entry, source_ref, total_ref, kernel_ref, g):
    target, place, side = entry
    rows = source_ref[place, pl.ds(pl.multiple_of(side * 32, 32), 32), :]
    values = jnp.concatenate([rows[:SIDES], rows[SIDES:]], axis=1)
    total_ref[target] += jnp.dot(values, kernel_ref[g], preferred_element_type=jnp.float32)


def work(groups, entry, source_ref, feature_ref, total_ref, square_ref, kernel_ref):
    for g in range(GROUP):
        start_pair(entry(g), source_ref, feature_ref, square_ref, g)

    def body(k, carry):
        for half in range(2):
            at = (2 * k + half) * GROUP
            mine = half * GROUP
            for g in range(GROUP):
                start_pair(
                    entry(at + GROUP + g), source_ref, feature_ref, square_ref, GROUP - mine + g
                )
                values_of_pair(square_ref, kernel_ref, mine + g)
                if g:
                    finish_pair(entry(at + g - 1), source_ref, total_ref, kernel_ref, mine + g - 1)
            finish_pair(entry(at + GROUP - 1), source_ref, total_ref, kernel_ref, mine + GROUP - 1)
        return carry

    lax.fori_loop(0, groups, body, 0)


def own_kernel(place_ref, table_ref, feature_ref, total_ref, list_ref, square_ref, kernel_ref):
    listed, boxes = place_ref.shape
    total_ref[...] = jnp.zeros_like(total_ref)

    def entry(k):
        b = jnp.minimum(k, boxes - 1)
        return b, shifted(b, PART), b & (PART - 1)

    groups = boxes // (2 * GROUP)
    work(groups, entry, table_ref, feature_ref, total_ref, square_ref, kernel_ref)

    parts = list_ref.shape[0]

    def scan(b, counts):
        counts = list(counts)
        for i in range(listed):
            place = place_ref[i, b]
            part = shifted(place & (SLOTS - 1), PART)
            code = b * 1024 + place
            for c in range(parts):
                list_ref[c, counts[c]] = code
                counts[c] = counts[c] + jnp.where(part == c, 1, 0)
        return tuple(counts)

    counts = lax.fori_loop(0, boxes, scan, (jnp.int32(0),) * parts)
    for c in range(parts):
        for k in range(3 * GROUP):
            list_ref[c, counts[c] + k] = boxes * 1024
        list_ref[c, list_ref.shape[1] - 1] = (counts[c] + 2 * GROUP - 1) // (2 * GROUP)


def near_pairs(part, list_ref, got_ref, feature_ref, total_ref, square_ref, kernel_ref):
    def entry(k):
        code = list_ref[part, k]
        return shifted(code, 1024), shifted(code & 1023, SLOTS), code & (PART - 1)

    groups = list_ref[part, list_ref.shape[1] - 1]
    work(groups, entry, got_ref, feature_ref, total_ref, square_ref, kernel_ref)


def near_kernel(part, list_ref, got_ref, feature_ref, old_ref, total_ref, square_ref, kernel_ref):
    total_ref[...] = old_ref[...]
    near_pairs(part, list_ref, got_ref, feature_ref, total_ref, square_ref, kernel_ref)


def last_kernel(
    part, list_ref, code0_ref, code1_ref,
    got_hbm, feature_hbm, old_hbm, table_hbm, couple0_hbm, couple1_hbm, transfer_hbm, basis_hbm,
    out_ref,
    got_ref, feature_ref, near_ref, table_ref, couple0_ref, couple1_ref, transfer_ref, basis_ref,
    square_ref, kernel_ref, stack_ref, up_ref, sems,
):
    listed = code0_ref.shape[1]
    parents = transfer_ref.shape[0]
    length = listed * WIDTH
    lane = lax.broadcasted_iota(jnp.int32, (SIDES, HALF), 1)
    pairs = [
        (got_hbm, got_ref), (feature_hbm, feature_ref), (old_hbm, near_ref),
        (table_hbm, table_ref), (transfer_hbm, transfer_ref), (couple1_hbm, couple1_ref),
        (basis_hbm, basis_ref), (couple0_hbm, couple0_ref),
    ]
    copies = [pltpu.make_async_copy(a, b, sems.at[i]) for i, (a, b) in enumerate(pairs)]
    for copy in copies:
        copy.start()
    for copy in copies[:3]:
        copy.wait()
    near_pairs(part, list_ref, got_ref, feature_ref, near_ref, square_ref, kernel_ref)
    for copy in copies[3:]:
        copy.wait()

    def piece(code_ref, row, j):
        code = code_ref[row, j]
        tile = table_ref[shifted(code, 2)]
        return jnp.where(((code + j) & 1) == 0, tile, pltpu.roll(tile, WIDTH, 1))

    def gather(code_ref, row, into_ref, at):
        for j in range(0, listed, 2):
            tile = piece(code_ref, row, j)
            if j + 1 < listed:
                tile = jnp.where(lane < WIDTH, tile, piece(code_ref, row, j + 1))
            into_ref[at : at + SIDES, j * WIDTH : (j + 2) * WIDTH] = tile

    def gather_parent(p):
        gather(code1_ref, p, up_ref.at[p % 2], 0)
        for i in range(8):
            gather(code0_ref, 8 * p + i, stack_ref.at[p % 2], i * SIDES)

    gather_parent(0)
    for p in range(parents):
        if p + 1 < parents:
            gather_parent(p + 1)
        parent_far = contract_last(up_ref[p % 2, :, :length], couple1_ref[p]).astype(jnp.bfloat16)
        down = jnp.dot(parent_far, transfer_ref[p], preferred_element_type=jnp.float32)
        for half in range(2):
            first = 8 * p + 4 * half
            matrices = couple0_ref[first : first + 4].reshape(4 * WIDTH, length)
            stacked = stack_ref[p % 2, 4 * half * SIDES : 4 * (half + 1) * SIDES, :length]
            product = contract_last(stacked, matrices)
            for k in range(4):
                i = 4 * half + k
                field = (
                    product[k * SIDES : (k + 1) * SIDES, k * WIDTH : (k + 1) * WIDTH]
                    + down[:, i * WIDTH : (i + 1) * WIDTH]
                ).astype(jnp.bfloat16)
                far = jnp.dot(field, basis_ref[first + k], preferred_element_type=jnp.float32)
                at = (first + k) * LEAF
                out_ref[:, at : at + LEAF] = (far + near_ref[first + k]).astype(jnp.bfloat16)


def on_device(
    x_values, coords, weights, basis, transfer, couple0, couple1,
    first_far_partner_device, far0_box, far1_dev, far1_box, near_partner_device, near_box,
):
    devices = lax.axis_size(AXES)
    boxes = basis.shape[0]
    parents = transfer.shape[0]
    listed = near_partner_device.shape[1]

    def params(mib):
        return pltpu.CompilerParams(vmem_limit_bytes=mib * 2**20)

    rows = boxes // 2 + parents // 2

    coef, asked, place = pl.pallas_call(
        first_kernel,
        out_shape=(
            jax.ShapeDtypeStruct((rows, SIDES, HALF), jnp.bfloat16),
            jax.ShapeDtypeStruct((devices, devices), jnp.int32),
            jax.ShapeDtypeStruct((listed, boxes), jnp.int32),
        ),
        in_specs=[hbm()] * 5,
        out_specs=(vmem(), vmem(), vmem()),
        scratch_shapes=[
            pltpu.VMEM(x_values.shape, jnp.bfloat16),
            pltpu.VMEM(basis.shape, jnp.bfloat16),
            pltpu.VMEM(transfer.shape, jnp.bfloat16),
            pltpu.VMEM((listed, boxes), jnp.int32),
            pltpu.VMEM((listed, boxes), jnp.int32),
            pltpu.SemaphoreType.DMA((4 + boxes // 8,)),
        ],
        compiler_params=params(60),
        name="first",
    )(x_values, basis, transfer, near_partner_device.T, near_box.T)
    table = lax.all_gather(coef, AXES, axis=0, tiled=True)
    requests = lax.all_to_all(
        asked.reshape(devices, 1, devices), AXES, split_axis=0, concat_axis=0, tiled=True
    ).reshape(devices, devices)

    halves = coords.reshape(3, boxes, 2, HALF).transpose(1, 2, 0, 3)
    source = jnp.pad(halves, ((0, 0), (0, 0), (0, 1), (0, 0)), constant_values=0.5)
    source = source.reshape(boxes // PART, 8 * PART, HALF)
    target = jnp.pad(coords.reshape(3, boxes, LEAF), ((0, 1), (0, 0), (0, 0)), constant_values=0.5)
    target = target.transpose(1, 0, 2)
    target = jnp.concatenate([target, target], axis=1)
    own, coded, features = pl.pallas_call(
        prepare_kernel,
        out_shape=(
            jax.ShapeDtypeStruct((boxes // PART, ROWS, HALF), jnp.bfloat16),
            jax.ShapeDtypeStruct((boxes, 8, HALF), jnp.float32),
            jax.ShapeDtypeStruct((boxes + 1, FEATURES, 2 * LEAF), jnp.bfloat16),
        ),
        in_specs=[vmem()] * 4,
        out_specs=(vmem(), vmem(), vmem()),
        compiler_params=params(8),
        name="prepare",
    )(x_values, weights.reshape(1, boxes * LEAF), source, target)

    scratch = [
        pltpu.VMEM((2 * GROUP, HALF, 2 * LEAF), jnp.float32),
        pltpu.VMEM((2 * GROUP, LEAF, LEAF), jnp.bfloat16),
    ]
    parts = SLOTS // PART
    pairs = boxes * LEAF * LEAF
    per_step = 16

    def pack(part):
        return pl.pallas_call(
            functools.partial(pack_kernel, part),
            out_shape=jax.ShapeDtypeStruct((devices, ROWS, HALF), jnp.bfloat16),
            grid=(devices // per_step,),
            in_specs=[
                smem(),
                pl.BlockSpec((boxes // PART, ROWS, HALF), lambda i: (0, 0, 0)),
                pl.BlockSpec((boxes, 8, HALF), lambda i: (0, 0, 0)),
            ],
            out_specs=pl.BlockSpec((per_step, ROWS, HALF), lambda i: (i, 0, 0)),
            compiler_params=params(59),
            name="pack",
        )(requests, own, coded)

    packed = [pack(0)]
    packed[0], requests, place = lax.optimization_barrier((packed[0], requests, place))
    packed += [pack(part) for part in range(1, parts)]
    total_shape = jax.ShapeDtypeStruct((boxes + 1, SIDES, LEAF), jnp.float32)
    near, listing = pl.pallas_call(
        own_kernel,
        out_shape=(total_shape, jax.ShapeDtypeStruct((parts, 384), jnp.int32)),
        in_specs=[smem(), vmem(), vmem()],
        out_specs=(vmem(), smem()),
        scratch_shapes=scratch,
        compiler_params=params(12),
        cost_estimate=pl.CostEstimate(
            flops=40 * pairs, bytes_accessed=4 << 20, transcendentals=2 * pairs
        ),
        name="own",
    )(place, own, features)
    later, listing = lax.optimization_barrier((packed[1:], listing))
    packed = [packed[0], *later]

    for part in range(parts):
        got = lax.all_to_all(packed[part], AXES, split_axis=0, concat_axis=0, tiled=True)
        if part == parts - 1:
            break
        near = pl.pallas_call(
            functools.partial(near_kernel, part),
            out_shape=total_shape,
            in_specs=[smem(), vmem(), vmem(), vmem()],
            out_specs=vmem(),
            scratch_shapes=scratch,
            input_output_aliases={3: 0},
            compiler_params=params(12),
            cost_estimate=pl.CostEstimate(
                flops=160 * pairs, bytes_accessed=8 << 20, transcendentals=8 * pairs
            ),
            name="near",
        )(listing, got, features, near)

    padded = (couple0.shape[2] + HALF - 1) // HALF * HALF
    held = [got, features, near, table, couple0, couple1, transfer, basis]
    return pl.pallas_call(
        functools.partial(last_kernel, parts - 1),
        out_shape=jax.ShapeDtypeStruct((SIDES, boxes * LEAF), jnp.bfloat16),
        in_specs=[smem()] * 3 + [hbm()] * len(held),
        out_specs=vmem(),
        scratch_shapes=[pltpu.VMEM(a.shape, a.dtype) for a in held]
        + scratch
        + [
            pltpu.VMEM((2, 8 * SIDES, padded), jnp.bfloat16),
            pltpu.VMEM((2, SIDES, padded), jnp.bfloat16),
            pltpu.SemaphoreType.DMA((len(held),)),
        ],
        compiler_params=params(59),
        name="last",
    )(
        listing,
        first_far_partner_device * (2 * rows) + far0_box,
        far1_dev * (2 * rows) + boxes + far1_box,
        *held,
    )


def solution(mesh):
    placed = (
        P(None, AXES),
        P(None, AXES),
        P(AXES),
        P(AXES, None, None),
        P(AXES, None, None),
        P(AXES, None, None),
        P(AXES, None, None),
        P(AXES, None),
        P(AXES, None),
        P(AXES, None),
        P(AXES, None),
        P(AXES, None),
        P(AXES, None),
    )
    return jax.shard_map(
        on_device, mesh=mesh, in_specs=placed, out_specs=P(None, AXES), check_vma=False
    )
```

```python
import functools
import math

import jax
import jax.numpy as jnp
import numpy as np
from jax import lax
from jax.experimental import pallas as pl
from jax.experimental.pallas import tpu as pltpu
from jax.sharding import PartitionSpec as P

AXES = ("row", "col")
LEAF = 256
HALF = 128
WIDTH = 64
SIDES = 16
SLOTS = 4
PART = 2
ROWS = 40 * PART
FEATURES = 48
GROUP = 8
BIAS = 1e-5
CODE = 248.0
CYCLES = 20.0 / (2.0 * math.pi)
SOFTEN = 0.01 * CYCLES * CYCLES


def cosine_polynomial(degree):
    fit = np.polynomial.chebyshev.Chebyshev.interpolate(
        lambda z: np.cos(2 * np.pi * np.sqrt(np.maximum(z, 0.0))), degree, [0.0, 0.25]
    )
    return [float(c) for c in fit.convert(kind=np.polynomial.Polynomial).coef]


COSINE = cosine_polynomial(4)
LEAD = COSINE[-1]
MONIC = [c / LEAD for c in COSINE[:-1]]
FOLD = LEAD * CYCLES


def split(value):
    high = value.astype(jnp.bfloat16).astype(jnp.float32)
    low = (value - high).astype(jnp.bfloat16).astype(jnp.float32)
    return high, low


def shifted(number, by):
    return lax.shift_right_logical(number, jnp.int32(by.bit_length() - 1))


def contract_last(a, b):
    return lax.dot_general(a, b, (((1,), (1,)), ((), ())), preferred_element_type=jnp.float32)


def vmem():
    return pl.BlockSpec(memory_space=pltpu.VMEM)


def hbm():
    return pl.BlockSpec(memory_space=pltpu.HBM)


def smem():
    return pl.BlockSpec(memory_space=pltpu.SMEM)


def plan(dev_ref, box_ref, asked_ref, place_ref):
    listed, count = dev_ref.shape
    devices = asked_ref.shape[0]
    owner = lax.broadcasted_iota(jnp.int32, (devices, count), 0)
    dev, box = dev_ref[...], box_ref[...]
    named = jnp.zeros((devices, count), jnp.float32)
    wanted = jnp.zeros((devices, count), jnp.float32)
    hits = []
    for i in range(listed):
        hit = (dev[i : i + 1] == owner).astype(jnp.float32)
        hits.append(hit)
        named = named + hit
        wanted = wanted + hit * box[i : i + 1].astype(jnp.float32)
    row = lax.broadcasted_iota(jnp.int32, (count, count), 0)
    col = lax.broadcasted_iota(jnp.int32, (count, count), 1)
    before = jnp.dot(
        named.astype(jnp.bfloat16),
        (row < col).astype(jnp.bfloat16),
        preferred_element_type=jnp.float32,
    )
    slot = lax.broadcasted_iota(jnp.int32, (devices, devices), 1)
    asked = jnp.zeros((devices, devices), jnp.float32)
    for p in range(SLOTS):
        here = jnp.sum(
            jnp.where((before == p) & (named > 0), wanted, 0.0), axis=1, keepdims=True
        )
        asked = jnp.where(slot == p, here, asked)
    asked_ref[...] = asked.astype(jnp.int32)
    position = [jnp.sum(hit * before, axis=0, keepdims=True) for hit in hits]
    place_ref[...] = dev * SLOTS + jnp.concatenate(position, axis=0).astype(jnp.int32)


def coefficients(x_ref, basis_ref, transfer_ref, out_ref, arrived):
    boxes = basis_ref.shape[0]
    parents = transfer_ref.shape[0]
    leaf, up = [], []
    for b in range(boxes):
        if b % 8 == 0:
            arrived(b // 8)
        leaf.append(contract_last(x_ref[:, b * LEAF : (b + 1) * LEAF], basis_ref[b]))
        if b % 2:
            out_ref[b // 2] = jnp.concatenate(leaf[b - 1 :], axis=1).astype(jnp.bfloat16)
    for p in range(parents):
        children = jnp.concatenate([out_ref[4 * p + i] for i in range(4)], axis=1)
        up.append(contract_last(children, transfer_ref[p]))
        if p % 2:
            out_ref[boxes // 2 + p // 2] = jnp.concatenate(up[p - 1 :], axis=1).astype(jnp.bfloat16)


def first_kernel(
    x_hbm, basis_hbm, transfer_hbm, dev_hbm, box_hbm, coef_ref, asked_ref, place_ref,
    x_ref, basis_ref, transfer_ref, dev_ref, box_ref, sems,
):
    lists = [
        pltpu.make_async_copy(dev_hbm, dev_ref, sems.at[0]),
        pltpu.make_async_copy(box_hbm, box_ref, sems.at[1]),
    ]
    arrays = [
        pltpu.make_async_copy(x_hbm, x_ref, sems.at[2]),
        pltpu.make_async_copy(transfer_hbm, transfer_ref, sems.at[3]),
    ]
    eights = [
        pltpu.make_async_copy(
            basis_hbm.at[8 * i : 8 * i + 8], basis_ref.at[8 * i : 8 * i + 8], sems.at[4 + i]
        )
        for i in range(basis_ref.shape[0] // 8)
    ]
    for copy in lists + arrays + eights:
        copy.start()
    for copy in lists:
        copy.wait()
    plan(dev_ref, box_ref, asked_ref, place_ref)
    for copy in arrays:
        copy.wait()
    coefficients(x_ref, basis_ref, transfer_ref, coef_ref, lambda i: eights[i].wait())


def prepare_kernel(
    x_ref, weight_ref, source_ref, target_ref, table_ref, coded_ref, feature_ref
):
    boxes = target_ref.shape[0]
    for b in range(boxes):
        for h in range(2):
            at = b * LEAF + h * HALF
            values = x_ref[:, at : at + HALF].astype(jnp.float32)
            scaled = values * (weight_ref[0:1, at : at + HALF] * FOLD)
            first = (b % PART) * 32 + h * SIDES
            table_ref[b // PART, first : first + SIDES, :] = scaled.astype(jnp.bfloat16)
    for q in range(boxes // PART):
        coded = jnp.exp2(CODE * (source_ref[q] - 0.5)).astype(jnp.bfloat16)
        table_ref[q, 32 * PART :, :] = coded
        for p in range(PART):
            coded_ref[PART * q + p] = coded.astype(jnp.float32)[8 * p : 8 * (p + 1)]

    sub = lax.broadcasted_iota(jnp.int32, (8, LEAF), 0)

    def one(b, carry):
        point = (target_ref[b] - 0.5) * CYCLES
        high, low = split(point)
        whole = high + low
        square = whole * whole
        norm = square[0:1] + square[1:2] + square[2:3] + BIAS
        n1 = norm.astype(jnp.bfloat16).astype(jnp.float32)
        n2, n3 = split(norm - n1)
        last = jnp.where(sub == 0, n1, jnp.where(sub == 1, n2, jnp.where(sub == 2, n3, 0.0)))
        for h in range(2):
            here = (sub >= 4 * h) & (sub < 4 * h + 3)
            one_row = jnp.where(sub == 4 * h + 3, 1.0, 0.0)
            blocks = [
                jnp.where(here, -2.0 * high, one_row),
                jnp.where(here, -2.0 * low, one_row),
                jnp.where(here, -2.0 * high, one_row),
                jnp.where(here, -2.0 * low, 0.0),
                last,
                jnp.zeros_like(last),
            ]
            feature_ref[b, :, h * LEAF : (h + 1) * LEAF] = jnp.concatenate(blocks, 0).astype(
                jnp.bfloat16
            )
        return carry

    lax.fori_loop(0, boxes, one, 0)


def pack_kernel(part, asked_ref, table_ref, coded_ref, out_ref):
    step = pl.program_id(0)
    block = out_ref.shape[0]

    def one(k, carry):
        for d in [4 * k + i for i in range(4)]:
            coded = []
            for p in range(PART):
                q = asked_ref[step * block + d, part * PART + p]
                side = pl.multiple_of((q & (PART - 1)) * 32, 32)
                out_ref[d, 32 * p : 32 * (p + 1), :] = table_ref[
                    shifted(q, PART), pl.ds(side, 32), :
                ]
                coded.append(coded_ref[q])
            out_ref[d, 32 * PART :, :] = jnp.concatenate(coded, 0).astype(jnp.bfloat16)
        return carry

    lax.fori_loop(0, block // 4, one, 0)


def start_pair(entry, source_ref, feature_ref, square_ref, g):
    target, place, side = entry
    sub = lax.broadcasted_iota(jnp.int32, (8, HALF), 0)
    norm_row = (sub % 4) == 3
    both = source_ref[place, 32 * PART :, :].astype(jnp.float32)
    coded = jnp.where(side == 0, both[0:8], both[8:16])
    point = jnp.log2(coded) * (CYCLES / CODE)
    high, low = split(point)
    whole = high + low
    square = whole * whole
    norm = pltpu.roll(square, 1, 0) + pltpu.roll(square, 2, 0) + pltpu.roll(square, 3, 0)
    n1 = norm.astype(jnp.bfloat16).astype(jnp.float32)
    n2, n3 = split(norm - n1)
    ones = jnp.ones_like(norm)
    blocks = [
        jnp.where(norm_row, n1, high),
        jnp.where(norm_row, n2, high),
        jnp.where(norm_row, n3, low),
        low,
        ones,
        ones,
    ]
    features = jnp.concatenate(blocks, 0).T.astype(jnp.bfloat16)
    square_ref[g] = jnp.dot(features, feature_ref[target], preferred_element_type=jnp.float32)


def values_of_pair(square_ref, kernel_ref, g):
    for h in range(2):
        for r in range(0, HALF, 32):
            d = square_ref[g, r : r + 32, h * LEAF : (h + 1) * LEAF]
            turns = d * lax.rsqrt(d)
            turns = turns - jnp.round(turns)
            z = turns * turns
            value = z + MONIC[-1]
            for c in MONIC[-2::-1]:
                value = value * z + c
            value = value * lax.rsqrt(d + SOFTEN)
            kernel_ref[g, h * HALF + r : h * HALF + r + 32, :] = value.astype(jnp.bfloat16)


def finish_pair(entry, source_ref, total_ref, kernel_ref, g):
    target, place, side = entry
    rows = source_ref[place, pl.ds(pl.multiple_of(side * 32, 32), 32), :]
    values = jnp.concatenate([rows[:SIDES], rows[SIDES:]], axis=1)
    total_ref[target] += jnp.dot(values, kernel_ref[g], preferred_element_type=jnp.float32)


def work(groups, entry, source_ref, feature_ref, total_ref, square_ref, kernel_ref):
    for g in range(GROUP):
        start_pair(entry(g), source_ref, feature_ref, square_ref, g)

    def body(k, carry):
        for half in range(2):
            at = (2 * k + half) * GROUP
            mine = half * GROUP
            for g in range(GROUP):
                start_pair(
                    entry(at + GROUP + g), source_ref, feature_ref, square_ref, GROUP - mine + g
                )
                values_of_pair(square_ref, kernel_ref, mine + g)
                if g:
                    finish_pair(entry(at + g - 1), source_ref, total_ref, kernel_ref, mine + g - 1)
            finish_pair(entry(at + GROUP - 1), source_ref, total_ref, kernel_ref, mine + GROUP - 1)
        return carry

    lax.fori_loop(0, groups, body, 0)


def own_kernel(place_ref, table_ref, feature_ref, total_ref, list_ref, square_ref, kernel_ref):
    listed, boxes = place_ref.shape
    total_ref[...] = jnp.zeros_like(total_ref)

    def entry(k):
        b = jnp.minimum(k, boxes - 1)
        return b, shifted(b, PART), b & (PART - 1)

    groups = boxes // (2 * GROUP)
    work(groups, entry, table_ref, feature_ref, total_ref, square_ref, kernel_ref)

    parts = list_ref.shape[0]

    def scan(b, counts):
        counts = list(counts)
        for i in range(listed):
            place = place_ref[i, b]
            part = shifted(place & (SLOTS - 1), PART)
            code = b * 1024 + place
            for c in range(parts):
                list_ref[c, counts[c]] = code
                counts[c] = counts[c] + jnp.where(part == c, 1, 0)
        return tuple(counts)

    counts = lax.fori_loop(0, boxes, scan, (jnp.int32(0),) * parts)
    for c in range(parts):
        for k in range(3 * GROUP):
            list_ref[c, counts[c] + k] = boxes * 1024
        list_ref[c, list_ref.shape[1] - 1] = (counts[c] + 2 * GROUP - 1) // (2 * GROUP)


def near_pairs(part, list_ref, got_ref, feature_ref, total_ref, square_ref, kernel_ref):
    def entry(k):
        code = list_ref[part, k]
        return shifted(code, 1024), shifted(code & 1023, SLOTS), code & (PART - 1)

    groups = list_ref[part, list_ref.shape[1] - 1]
    work(groups, entry, got_ref, feature_ref, total_ref, square_ref, kernel_ref)


def near_kernel(part, list_ref, got_ref, feature_ref, old_ref, total_ref, square_ref, kernel_ref):
    total_ref[...] = old_ref[...]
    near_pairs(part, list_ref, got_ref, feature_ref, total_ref, square_ref, kernel_ref)


def last_kernel(
    part, list_ref, code0_ref, code1_ref,
    got_hbm, feature_hbm, old_hbm, table_hbm, couple0_hbm, couple1_hbm, transfer_hbm, basis_hbm,
    out_ref,
    got_ref, feature_ref, near_ref, table_ref, couple0_ref, couple1_ref, transfer_ref, basis_ref,
    square_ref, kernel_ref, stack_ref, up_ref, sems,
):
    listed = code0_ref.shape[1]
    parents = transfer_ref.shape[0]
    length = listed * WIDTH
    lane = lax.broadcasted_iota(jnp.int32, (SIDES, HALF), 1)
    pairs = [
        (got_hbm, got_ref), (feature_hbm, feature_ref), (old_hbm, near_ref),
        (table_hbm, table_ref), (transfer_hbm, transfer_ref), (couple1_hbm, couple1_ref),
        (basis_hbm, basis_ref), (couple0_hbm, couple0_ref),
    ]
    copies = [pltpu.make_async_copy(a, b, sems.at[i]) for i, (a, b) in enumerate(pairs)]
    for copy in copies[:3]:
        copy.start()
    for copy in copies[:3]:
        copy.wait()
    for copy in copies[3:]:
        copy.start()
    near_pairs(part, list_ref, got_ref, feature_ref, near_ref, square_ref, kernel_ref)
    for copy in copies[3:]:
        copy.wait()

    def piece(code_ref, row, j):
        code = code_ref[row, j]
        tile = table_ref[shifted(code, 2)]
        return jnp.where(((code + j) & 1) == 0, tile, pltpu.roll(tile, WIDTH, 1))

    def gather(code_ref, row, into_ref, at):
        for j in range(0, listed, 2):
            tile = piece(code_ref, row, j)
            if j + 1 < listed:
                tile = jnp.where(lane < WIDTH, tile, piece(code_ref, row, j + 1))
            into_ref[at : at + SIDES, j * WIDTH : (j + 2) * WIDTH] = tile

    def gather_parent(p):
        gather(code1_ref, p, up_ref.at[p % 2], 0)
        for i in range(8):
            gather(code0_ref, 8 * p + i, stack_ref.at[p % 2], i * SIDES)

    gather_parent(0)
    for p in range(parents):
        if p + 1 < parents:
            gather_parent(p + 1)
        parent_far = contract_last(up_ref[p % 2, :, :length], couple1_ref[p]).astype(jnp.bfloat16)
        down = jnp.dot(parent_far, transfer_ref[p], preferred_element_type=jnp.float32)
        for half in range(2):
            first = 8 * p + 4 * half
            matrices = couple0_ref[first : first + 4].reshape(4 * WIDTH, length)
            stacked = stack_ref[p % 2, 4 * half * SIDES : 4 * (half + 1) * SIDES, :length]
            product = contract_last(stacked, matrices)
            for k in range(4):
                i = 4 * half + k
                field = (
                    product[k * SIDES : (k + 1) * SIDES, k * WIDTH : (k + 1) * WIDTH]
                    + down[:, i * WIDTH : (i + 1) * WIDTH]
                ).astype(jnp.bfloat16)
                far = jnp.dot(field, basis_ref[first + k], preferred_element_type=jnp.float32)
                at = (first + k) * LEAF
                out_ref[:, at : at + LEAF] = (far + near_ref[first + k]).astype(jnp.bfloat16)


def on_device(
    x_values, coords, weights, basis, transfer, couple0, couple1,
    first_far_partner_device, far0_box, far1_dev, far1_box, near_partner_device, near_box,
):
    devices = lax.axis_size(AXES)
    boxes = basis.shape[0]
    parents = transfer.shape[0]
    listed = near_partner_device.shape[1]

    def params(mib):
        return pltpu.CompilerParams(vmem_limit_bytes=mib * 2**20)

    rows = boxes // 2 + parents // 2

    coef, asked, place = pl.pallas_call(
        first_kernel,
        out_shape=(
            jax.ShapeDtypeStruct((rows, SIDES, HALF), jnp.bfloat16),
            jax.ShapeDtypeStruct((devices, devices), jnp.int32),
            jax.ShapeDtypeStruct((listed, boxes), jnp.int32),
        ),
        in_specs=[hbm()] * 5,
        out_specs=(vmem(), vmem(), vmem()),
        scratch_shapes=[
            pltpu.VMEM(x_values.shape, jnp.bfloat16),
            pltpu.VMEM(basis.shape, jnp.bfloat16),
            pltpu.VMEM(transfer.shape, jnp.bfloat16),
            pltpu.VMEM((listed, boxes), jnp.int32),
            pltpu.VMEM((listed, boxes), jnp.int32),
            pltpu.SemaphoreType.DMA((4 + boxes // 8,)),
        ],
        compiler_params=params(60),
        name="first",
    )(x_values, basis, transfer, near_partner_device.T, near_box.T)
    table = lax.all_gather(coef, AXES, axis=0, tiled=True)
    requests = lax.all_to_all(
        asked.reshape(devices, 1, devices), AXES, split_axis=0, concat_axis=0, tiled=True
    ).reshape(devices, devices)

    halves = coords.reshape(3, boxes, 2, HALF).transpose(1, 2, 0, 3)
    source = jnp.pad(halves, ((0, 0), (0, 0), (0, 1), (0, 0)), constant_values=0.5)
    source = source.reshape(boxes // PART, 8 * PART, HALF)
    target = jnp.pad(coords.reshape(3, boxes, LEAF), ((0, 1), (0, 0), (0, 0)), constant_values=0.5)
    target = target.transpose(1, 0, 2)
    target = jnp.concatenate([target, target], axis=1)
    own, coded, features = pl.pallas_call(
        prepare_kernel,
        out_shape=(
            jax.ShapeDtypeStruct((boxes // PART, ROWS, HALF), jnp.bfloat16),
            jax.ShapeDtypeStruct((boxes, 8, HALF), jnp.float32),
            jax.ShapeDtypeStruct((boxes + 1, FEATURES, 2 * LEAF), jnp.bfloat16),
        ),
        in_specs=[vmem()] * 4,
        out_specs=(vmem(), vmem(), vmem()),
        compiler_params=params(8),
        name="prepare",
    )(x_values, weights.reshape(1, boxes * LEAF), source, target)

    scratch = [
        pltpu.VMEM((2 * GROUP, HALF, 2 * LEAF), jnp.float32),
        pltpu.VMEM((2 * GROUP, LEAF, LEAF), jnp.bfloat16),
    ]
    parts = SLOTS // PART
    pairs = boxes * LEAF * LEAF
    per_step = devices // 2

    def pack(part):
        return pl.pallas_call(
            functools.partial(pack_kernel, part),
            out_shape=jax.ShapeDtypeStruct((devices, ROWS, HALF), jnp.bfloat16),
            grid=(devices // per_step,),
            in_specs=[
                smem(),
                pl.BlockSpec((boxes // PART, ROWS, HALF), lambda i: (0, 0, 0)),
                pl.BlockSpec((boxes, 8, HALF), lambda i: (0, 0, 0)),
            ],
            out_specs=pl.BlockSpec((per_step, ROWS, HALF), lambda i: (i, 0, 0)),
            compiler_params=params(59),
            name="pack",
        )(requests, own, coded)

    packed = [pack(0)]
    packed[0], requests, place = lax.optimization_barrier((packed[0], requests, place))
    packed += [pack(part) for part in range(1, parts)]
    total_shape = jax.ShapeDtypeStruct((boxes + 1, SIDES, LEAF), jnp.float32)
    near, listing = pl.pallas_call(
        own_kernel,
        out_shape=(total_shape, jax.ShapeDtypeStruct((parts, 384), jnp.int32)),
        in_specs=[smem(), vmem(), vmem()],
        out_specs=(vmem(), smem()),
        scratch_shapes=scratch,
        compiler_params=params(12),
        cost_estimate=pl.CostEstimate(
            flops=40 * pairs, bytes_accessed=4 << 20, transcendentals=2 * pairs
        ),
        name="own",
    )(place, own, features)
    codes = (
        first_far_partner_device * (2 * rows) + far0_box,
        far1_dev * (2 * rows) + boxes + far1_box,
    )
    later, listing, codes = lax.optimization_barrier((packed[1:], listing, codes))
    packed = [packed[0], *later]

    for part in range(parts):
        got = lax.all_to_all(packed[part], AXES, split_axis=0, concat_axis=0, tiled=True)
        if part == parts - 1:
            break
        near = pl.pallas_call(
            functools.partial(near_kernel, part),
            out_shape=total_shape,
            in_specs=[smem(), vmem(), vmem(), vmem()],
            out_specs=vmem(),
            scratch_shapes=scratch,
            input_output_aliases={3: 0},
            compiler_params=params(12),
            cost_estimate=pl.CostEstimate(
                flops=160 * pairs, bytes_accessed=8 << 20, transcendentals=8 * pairs
            ),
            name="near",
        )(listing, got, features, near)

    padded = (couple0.shape[2] + HALF - 1) // HALF * HALF
    held = [got, features, near, table, couple0, couple1, transfer, basis]
    return pl.pallas_call(
        functools.partial(last_kernel, parts - 1),
        out_shape=jax.ShapeDtypeStruct((SIDES, boxes * LEAF), jnp.bfloat16),
        in_specs=[smem()] * 3 + [hbm()] * len(held),
        out_specs=vmem(),
        scratch_shapes=[pltpu.VMEM(a.shape, a.dtype) for a in held]
        + scratch
        + [
            pltpu.VMEM((2, 8 * SIDES, padded), jnp.bfloat16),
            pltpu.VMEM((2, SIDES, padded), jnp.bfloat16),
            pltpu.SemaphoreType.DMA((len(held),)),
        ],
        compiler_params=params(59),
        name="last",
    )(
        listing,
        *codes,
        *held,
    )


def solution(mesh):
    placed = (
        P(None, AXES),
        P(None, AXES),
        P(AXES),
        P(AXES, None, None),
        P(AXES, None, None),
        P(AXES, None, None),
        P(AXES, None, None),
        P(AXES, None),
        P(AXES, None),
        P(AXES, None),
        P(AXES, None),
        P(AXES, None),
        P(AXES, None),
    )
    return jax.shard_map(
        on_device, mesh=mesh, in_specs=placed, out_specs=P(None, AXES), check_vma=False
    )
```

```python
import functools
import math

import jax
import jax.numpy as jnp
import numpy as np
from jax import lax
from jax.experimental import pallas as pl
from jax.experimental.pallas import tpu as pltpu
from jax.sharding import PartitionSpec as P

AXES = ("row", "col")
LEAF = 256
HALF = 128
WIDTH = 64
SIDES = 16
SLOTS = 4
PART = 2
ROWS = 40 * PART
FEATURES = 48
GROUP = 8
BIAS = 1e-5
CODE = 248.0
CYCLES = 20.0 / (2.0 * math.pi)
SOFTEN = 0.01 * CYCLES * CYCLES


def cosine_polynomial(degree):
    fit = np.polynomial.chebyshev.Chebyshev.interpolate(
        lambda z: np.cos(2 * np.pi * np.sqrt(np.maximum(z, 0.0))), degree, [0.0, 0.25]
    )
    return [float(c) for c in fit.convert(kind=np.polynomial.Polynomial).coef]


COSINE = cosine_polynomial(4)
LEAD = COSINE[-1]
MONIC = [c / LEAD for c in COSINE[:-1]]
FOLD = LEAD * CYCLES


def split(value):
    high = value.astype(jnp.bfloat16).astype(jnp.float32)
    low = (value - high).astype(jnp.bfloat16).astype(jnp.float32)
    return high, low


def shifted(number, by):
    return lax.shift_right_logical(number, jnp.int32(by.bit_length() - 1))


def contract_last(a, b):
    return lax.dot_general(a, b, (((1,), (1,)), ((), ())), preferred_element_type=jnp.float32)


def vmem():
    return pl.BlockSpec(memory_space=pltpu.VMEM)


def hbm():
    return pl.BlockSpec(memory_space=pltpu.HBM)


def smem():
    return pl.BlockSpec(memory_space=pltpu.SMEM)


def plan(dev_ref, box_ref, asked_ref, place_ref):
    listed, count = dev_ref.shape
    devices = asked_ref.shape[0]
    owner = lax.broadcasted_iota(jnp.int32, (devices, count), 0)
    dev, box = dev_ref[...], box_ref[...]
    named = jnp.zeros((devices, count), jnp.float32)
    wanted = jnp.zeros((devices, count), jnp.float32)
    hits = []
    for i in range(listed):
        hit = (dev[i : i + 1] == owner).astype(jnp.float32)
        hits.append(hit)
        named = named + hit
        wanted = wanted + hit * box[i : i + 1].astype(jnp.float32)
    row = lax.broadcasted_iota(jnp.int32, (count, count), 0)
    col = lax.broadcasted_iota(jnp.int32, (count, count), 1)
    before = jnp.dot(
        named.astype(jnp.bfloat16),
        (row < col).astype(jnp.bfloat16),
        preferred_element_type=jnp.float32,
    )
    slot = lax.broadcasted_iota(jnp.int32, (devices, devices), 1)
    asked = jnp.zeros((devices, devices), jnp.float32)
    for p in range(SLOTS):
        here = jnp.sum(
            jnp.where((before == p) & (named > 0), wanted, 0.0), axis=1, keepdims=True
        )
        asked = jnp.where(slot == p, here, asked)
    asked_ref[...] = asked.astype(jnp.int32)
    position = [jnp.sum(hit * before, axis=0, keepdims=True) for hit in hits]
    place_ref[...] = dev * SLOTS + jnp.concatenate(position, axis=0).astype(jnp.int32)


def coefficients(x_ref, basis_ref, transfer_ref, out_ref, arrived):
    boxes = basis_ref.shape[0]
    parents = transfer_ref.shape[0]
    leaf, up = [], []
    for b in range(boxes):
        if b % 8 == 0:
            arrived(b // 8)
        leaf.append(contract_last(x_ref[:, b * LEAF : (b + 1) * LEAF], basis_ref[b]))
        if b % 2:
            out_ref[b // 2] = jnp.concatenate(leaf[b - 1 :], axis=1).astype(jnp.bfloat16)
    for p in range(parents):
        children = jnp.concatenate([out_ref[4 * p + i] for i in range(4)], axis=1)
        up.append(contract_last(children, transfer_ref[p]))
        if p % 2:
            out_ref[boxes // 2 + p // 2] = jnp.concatenate(up[p - 1 :], axis=1).astype(jnp.bfloat16)


def first_kernel(
    x_hbm, basis_hbm, transfer_hbm, dev_hbm, box_hbm, coef_ref, asked_ref, place_ref,
    x_ref, basis_ref, transfer_ref, dev_ref, box_ref, sems,
):
    lists = [
        pltpu.make_async_copy(dev_hbm, dev_ref, sems.at[0]),
        pltpu.make_async_copy(box_hbm, box_ref, sems.at[1]),
    ]
    arrays = [
        pltpu.make_async_copy(x_hbm, x_ref, sems.at[2]),
        pltpu.make_async_copy(transfer_hbm, transfer_ref, sems.at[3]),
    ]
    eights = [
        pltpu.make_async_copy(
            basis_hbm.at[8 * i : 8 * i + 8], basis_ref.at[8 * i : 8 * i + 8], sems.at[4 + i]
        )
        for i in range(basis_ref.shape[0] // 8)
    ]
    for copy in lists + arrays + eights:
        copy.start()
    for copy in lists:
        copy.wait()
    plan(dev_ref, box_ref, asked_ref, place_ref)
    for copy in arrays:
        copy.wait()
    coefficients(x_ref, basis_ref, transfer_ref, coef_ref, lambda i: eights[i].wait())


def prepare_kernel(
    x_ref, weight_ref, source_ref, target_ref, table_ref, coded_ref, feature_ref
):
    boxes = target_ref.shape[0]
    for b in range(boxes):
        for h in range(2):
            at = b * LEAF + h * HALF
            values = x_ref[:, at : at + HALF].astype(jnp.float32)
            scaled = values * (weight_ref[0:1, at : at + HALF] * FOLD)
            first = (b % PART) * 32 + h * SIDES
            table_ref[b // PART, first : first + SIDES, :] = scaled.astype(jnp.bfloat16)
    for q in range(boxes // PART):
        coded = jnp.exp2(CODE * (source_ref[q] - 0.5)).astype(jnp.bfloat16)
        table_ref[q, 32 * PART :, :] = coded
        for p in range(PART):
            coded_ref[PART * q + p] = coded.astype(jnp.float32)[8 * p : 8 * (p + 1)]

    sub = lax.broadcasted_iota(jnp.int32, (8, LEAF), 0)

    def one(b, carry):
        point = (target_ref[b] - 0.5) * CYCLES
        high, low = split(point)
        whole = high + low
        square = whole * whole
        norm = square[0:1] + square[1:2] + square[2:3] + BIAS
        n1 = norm.astype(jnp.bfloat16).astype(jnp.float32)
        n2, n3 = split(norm - n1)
        last = jnp.where(sub == 0, n1, jnp.where(sub == 1, n2, jnp.where(sub == 2, n3, 0.0)))
        for h in range(2):
            here = (sub >= 4 * h) & (sub < 4 * h + 3)
            one_row = jnp.where(sub == 4 * h + 3, 1.0, 0.0)
            blocks = [
                jnp.where(here, -2.0 * high, one_row),
                jnp.where(here, -2.0 * low, one_row),
                jnp.where(here, -2.0 * high, one_row),
                jnp.where(here, -2.0 * low, 0.0),
                last,
                jnp.zeros_like(last),
            ]
            feature_ref[b, :, h * LEAF : (h + 1) * LEAF] = jnp.concatenate(blocks, 0).astype(
                jnp.bfloat16
            )
        return carry

    lax.fori_loop(0, boxes, one, 0)


def pack_kernel(part, asked_ref, table_ref, coded_ref, out_ref):
    step = pl.program_id(0)
    block = out_ref.shape[0]

    def one(k, carry):
        for d in [4 * k + i for i in range(4)]:
            coded = []
            for p in range(PART):
                q = asked_ref[step * block + d, part * PART + p]
                side = pl.multiple_of((q & (PART - 1)) * 32, 32)
                out_ref[d, 32 * p : 32 * (p + 1), :] = table_ref[
                    shifted(q, PART), pl.ds(side, 32), :
                ]
                coded.append(coded_ref[q])
            out_ref[d, 32 * PART :, :] = jnp.concatenate(coded, 0).astype(jnp.bfloat16)
        return carry

    lax.fori_loop(0, block // 4, one, 0)


def start_pair(entry, source_ref, feature_ref, square_ref, g):
    target, place, side = entry
    sub = lax.broadcasted_iota(jnp.int32, (8, HALF), 0)
    norm_row = (sub % 4) == 3
    both = source_ref[place, 32 * PART :, :].astype(jnp.float32)
    coded = jnp.where(side == 0, both[0:8], both[8:16])
    point = jnp.log2(coded) * (CYCLES / CODE)
    high, low = split(point)
    whole = high + low
    square = whole * whole
    norm = pltpu.roll(square, 1, 0) + pltpu.roll(square, 2, 0) + pltpu.roll(square, 3, 0)
    n1 = norm.astype(jnp.bfloat16).astype(jnp.float32)
    n2, n3 = split(norm - n1)
    ones = jnp.ones_like(norm)
    blocks = [
        jnp.where(norm_row, n1, high),
        jnp.where(norm_row, n2, high),
        jnp.where(norm_row, n3, low),
        low,
        ones,
        ones,
    ]
    features = jnp.concatenate(blocks, 0).T.astype(jnp.bfloat16)
    square_ref[g] = jnp.dot(features, feature_ref[target], preferred_element_type=jnp.float32)


def values_of_pair(square_ref, kernel_ref, g):
    for h in range(2):
        for r in range(0, HALF, 32):
            d = square_ref[g, r : r + 32, h * LEAF : (h + 1) * LEAF]
            turns = d * lax.rsqrt(d)
            turns = turns - jnp.round(turns)
            z = turns * turns
            value = z + MONIC[-1]
            for c in MONIC[-2::-1]:
                value = value * z + c
            value = value * lax.rsqrt(d + SOFTEN)
            kernel_ref[g, h * HALF + r : h * HALF + r + 32, :] = value.astype(jnp.bfloat16)


def finish_pair(entry, source_ref, total_ref, kernel_ref, g):
    target, place, side = entry
    rows = source_ref[place, pl.ds(pl.multiple_of(side * 32, 32), 32), :]
    values = jnp.concatenate([rows[:SIDES], rows[SIDES:]], axis=1)
    total_ref[target] += jnp.dot(values, kernel_ref[g], preferred_element_type=jnp.float32)


def work(groups, entry, source_ref, feature_ref, total_ref, square_ref, kernel_ref):
    for g in range(GROUP):
        start_pair(entry(g), source_ref, feature_ref, square_ref, g)

    def body(k, carry):
        for half in range(2):
            at = (2 * k + half) * GROUP
            mine = half * GROUP
            for g in range(GROUP):
                start_pair(
                    entry(at + GROUP + g), source_ref, feature_ref, square_ref, GROUP - mine + g
                )
                values_of_pair(square_ref, kernel_ref, mine + g)
                if g:
                    finish_pair(entry(at + g - 1), source_ref, total_ref, kernel_ref, mine + g - 1)
            finish_pair(entry(at + GROUP - 1), source_ref, total_ref, kernel_ref, mine + GROUP - 1)
        return carry

    lax.fori_loop(0, groups, body, 0)


def own_kernel(place_ref, table_ref, feature_ref, total_ref, list_ref, square_ref, kernel_ref):
    listed, boxes = place_ref.shape
    total_ref[...] = jnp.zeros_like(total_ref)

    def entry(k):
        b = jnp.minimum(k, boxes - 1)
        return b, shifted(b, PART), b & (PART - 1)

    groups = boxes // (2 * GROUP)
    work(groups, entry, table_ref, feature_ref, total_ref, square_ref, kernel_ref)

    parts = list_ref.shape[0]

    def scan(b, counts):
        counts = list(counts)
        for i in range(listed):
            place = place_ref[i, b]
            part = shifted(place & (SLOTS - 1), PART)
            code = b * 1024 + place
            for c in range(parts):
                list_ref[c, counts[c]] = code
                counts[c] = counts[c] + jnp.where(part == c, 1, 0)
        return tuple(counts)

    counts = lax.fori_loop(0, boxes, scan, (jnp.int32(0),) * parts)
    for c in range(parts):
        for k in range(3 * GROUP):
            list_ref[c, counts[c] + k] = boxes * 1024
        list_ref[c, list_ref.shape[1] - 1] = (counts[c] + 2 * GROUP - 1) // (2 * GROUP)


def near_pairs(part, list_ref, got_ref, feature_ref, total_ref, square_ref, kernel_ref):
    def entry(k):
        code = list_ref[part, k]
        return shifted(code, 1024), shifted(code & 1023, SLOTS), code & (PART - 1)

    groups = list_ref[part, list_ref.shape[1] - 1]
    work(groups, entry, got_ref, feature_ref, total_ref, square_ref, kernel_ref)


def near_kernel(part, list_ref, got_ref, feature_ref, old_ref, total_ref, square_ref, kernel_ref):
    total_ref[...] = old_ref[...]
    near_pairs(part, list_ref, got_ref, feature_ref, total_ref, square_ref, kernel_ref)


def last_kernel(
    part, list_ref, code0_ref, code1_ref,
    got_hbm, feature_hbm, old_hbm, table_hbm, couple0_hbm, couple1_hbm, transfer_hbm, basis_hbm,
    out_ref,
    got_ref, feature_ref, near_ref, table_ref, couple0_ref, couple1_ref, transfer_ref, basis_ref,
    square_ref, kernel_ref, stack_ref, up_ref, sems,
):
    listed = code0_ref.shape[1]
    parents = transfer_ref.shape[0]
    length = listed * WIDTH
    lane = lax.broadcasted_iota(jnp.int32, (SIDES, HALF), 1)
    pairs = [
        (got_hbm, got_ref), (feature_hbm, feature_ref), (old_hbm, near_ref),
        (table_hbm, table_ref), (transfer_hbm, transfer_ref), (couple1_hbm, couple1_ref),
        (basis_hbm, basis_ref), (couple0_hbm, couple0_ref),
    ]
    copies = [pltpu.make_async_copy(a, b, sems.at[i]) for i, (a, b) in enumerate(pairs)]
    for copy in copies:
        copy.start()
    for copy in copies[:3]:
        copy.wait()
    near_pairs(part, list_ref, got_ref, feature_ref, near_ref, square_ref, kernel_ref)
    for copy in copies[3:]:
        copy.wait()

    def piece(code_ref, row, j):
        code = code_ref[row, j]
        tile = table_ref[shifted(code, 2)]
        return jnp.where(((code + j) & 1) == 0, tile, pltpu.roll(tile, WIDTH, 1))

    def gather(code_ref, row, into_ref, at):
        for j in range(0, listed, 2):
            tile = piece(code_ref, row, j)
            if j + 1 < listed:
                tile = jnp.where(lane < WIDTH, tile, piece(code_ref, row, j + 1))
            into_ref[at : at + SIDES, j * WIDTH : (j + 2) * WIDTH] = tile

    def gather_parent(p):
        gather(code1_ref, p, up_ref.at[p % 2], 0)
        for i in range(8):
            gather(code0_ref, 8 * p + i, stack_ref.at[p % 2], i * SIDES)

    gather_parent(0)
    for p in range(parents):
        if p + 1 < parents:
            gather_parent(p + 1)
        parent_far = contract_last(up_ref[p % 2, :, :length], couple1_ref[p]).astype(jnp.bfloat16)
        down = jnp.dot(parent_far, transfer_ref[p], preferred_element_type=jnp.float32)
        for half in range(2):
            first = 8 * p + 4 * half
            matrices = couple0_ref[first : first + 4].reshape(4 * WIDTH, length)
            stacked = stack_ref[p % 2, 4 * half * SIDES : 4 * (half + 1) * SIDES, :length]
            product = contract_last(stacked, matrices)
            for k in range(4):
                i = 4 * half + k
                field = (
                    product[k * SIDES : (k + 1) * SIDES, k * WIDTH : (k + 1) * WIDTH]
                    + down[:, i * WIDTH : (i + 1) * WIDTH]
                ).astype(jnp.bfloat16)
                far = jnp.dot(field, basis_ref[first + k], preferred_element_type=jnp.float32)
                at = (first + k) * LEAF
                out_ref[:, at : at + LEAF] = (far + near_ref[first + k]).astype(jnp.bfloat16)


def on_device(
    x_values, coords, weights, basis, transfer, couple0, couple1,
    first_far_partner_device, far0_box, far1_dev, far1_box, near_partner_device, near_box,
):
    devices = lax.axis_size(AXES)
    boxes = basis.shape[0]
    parents = transfer.shape[0]
    listed = near_partner_device.shape[1]

    def params(mib):
        return pltpu.CompilerParams(vmem_limit_bytes=mib * 2**20)

    rows = boxes // 2 + parents // 2

    coef, asked, place = pl.pallas_call(
        first_kernel,
        out_shape=(
            jax.ShapeDtypeStruct((rows, SIDES, HALF), jnp.bfloat16),
            jax.ShapeDtypeStruct((devices, devices), jnp.int32),
            jax.ShapeDtypeStruct((listed, boxes), jnp.int32),
        ),
        in_specs=[hbm()] * 5,
        out_specs=(vmem(), vmem(), vmem()),
        scratch_shapes=[
            pltpu.VMEM(x_values.shape, jnp.bfloat16),
            pltpu.VMEM(basis.shape, jnp.bfloat16),
            pltpu.VMEM(transfer.shape, jnp.bfloat16),
            pltpu.VMEM((listed, boxes), jnp.int32),
            pltpu.VMEM((listed, boxes), jnp.int32),
            pltpu.SemaphoreType.DMA((4 + boxes // 8,)),
        ],
        compiler_params=params(60),
        name="first",
    )(x_values, basis, transfer, near_partner_device.T, near_box.T)
    table = lax.all_gather(coef, AXES, axis=0, tiled=True)
    requests = lax.all_to_all(
        asked.reshape(devices, 1, devices), AXES, split_axis=0, concat_axis=0, tiled=True
    ).reshape(devices, devices)

    halves = coords.reshape(3, boxes, 2, HALF).transpose(1, 2, 0, 3)
    source = jnp.pad(halves, ((0, 0), (0, 0), (0, 1), (0, 0)), constant_values=0.5)
    source = source.reshape(boxes // PART, 8 * PART, HALF)
    target = jnp.pad(coords.reshape(3, boxes, LEAF), ((0, 1), (0, 0), (0, 0)), constant_values=0.5)
    target = target.transpose(1, 0, 2)
    target = jnp.concatenate([target, target], axis=1)
    own, coded, features = pl.pallas_call(
        prepare_kernel,
        out_shape=(
            jax.ShapeDtypeStruct((boxes // PART, ROWS, HALF), jnp.bfloat16),
            jax.ShapeDtypeStruct((boxes, 8, HALF), jnp.float32),
            jax.ShapeDtypeStruct((boxes + 1, FEATURES, 2 * LEAF), jnp.bfloat16),
        ),
        in_specs=[vmem()] * 4,
        out_specs=(vmem(), vmem(), vmem()),
        compiler_params=params(8),
        name="prepare",
    )(x_values, weights.reshape(1, boxes * LEAF), source, target)

    scratch = [
        pltpu.VMEM((2 * GROUP, HALF, 2 * LEAF), jnp.float32),
        pltpu.VMEM((2 * GROUP, LEAF, LEAF), jnp.bfloat16),
    ]
    parts = SLOTS // PART
    pairs = boxes * LEAF * LEAF
    per_step = devices // 2

    def pack(part):
        return pl.pallas_call(
            functools.partial(pack_kernel, part),
            out_shape=jax.ShapeDtypeStruct((devices, ROWS, HALF), jnp.bfloat16),
            grid=(devices // per_step,),
            in_specs=[
                smem(),
                pl.BlockSpec((boxes // PART, ROWS, HALF), lambda i: (0, 0, 0)),
                pl.BlockSpec((boxes, 8, HALF), lambda i: (0, 0, 0)),
            ],
            out_specs=pl.BlockSpec((per_step, ROWS, HALF), lambda i: (i, 0, 0)),
            compiler_params=params(59),
            name="pack",
        )(requests, own, coded)

    packed = [pack(0)]
    packed[0], requests, place = lax.optimization_barrier((packed[0], requests, place))
    packed += [pack(part) for part in range(1, parts)]
    total_shape = jax.ShapeDtypeStruct((boxes + 1, SIDES, LEAF), jnp.float32)
    near, listing = pl.pallas_call(
        own_kernel,
        out_shape=(total_shape, jax.ShapeDtypeStruct((parts, 384), jnp.int32)),
        in_specs=[smem(), vmem(), vmem()],
        out_specs=(vmem(), smem()),
        scratch_shapes=scratch,
        compiler_params=params(12),
        cost_estimate=pl.CostEstimate(
            flops=40 * pairs, bytes_accessed=4 << 20, transcendentals=2 * pairs
        ),
        name="own",
    )(place, own, features)
    codes = (
        first_far_partner_device * (2 * rows) + far0_box,
        far1_dev * (2 * rows) + boxes + far1_box,
    )
    later, listing, codes = lax.optimization_barrier((packed[1:], listing, codes))
    packed = [packed[0], *later]

    for part in range(parts):
        got = lax.all_to_all(packed[part], AXES, split_axis=0, concat_axis=0, tiled=True)
        if part == parts - 1:
            break
        near = pl.pallas_call(
            functools.partial(near_kernel, part),
            out_shape=total_shape,
            in_specs=[smem(), vmem(), vmem(), vmem()],
            out_specs=vmem(),
            scratch_shapes=scratch,
            input_output_aliases={3: 0},
            compiler_params=params(12),
            cost_estimate=pl.CostEstimate(
                flops=160 * pairs, bytes_accessed=8 << 20, transcendentals=8 * pairs
            ),
            name="near",
        )(listing, got, features, near)

    padded = (couple0.shape[2] + HALF - 1) // HALF * HALF
    held = [got, features, near, table, couple0, couple1, transfer, basis]
    return pl.pallas_call(
        functools.partial(last_kernel, parts - 1),
        out_shape=jax.ShapeDtypeStruct((SIDES, boxes * LEAF), jnp.bfloat16),
        in_specs=[smem()] * 3 + [hbm()] * len(held),
        out_specs=vmem(),
        scratch_shapes=[pltpu.VMEM(a.shape, a.dtype) for a in held]
        + scratch
        + [
            pltpu.VMEM((2, 8 * SIDES, padded), jnp.bfloat16),
            pltpu.VMEM((2, SIDES, padded), jnp.bfloat16),
            pltpu.SemaphoreType.DMA((len(held),)),
        ],
        compiler_params=params(59),
        name="last",
    )(
        listing,
        *codes,
        *held,
    )


def solution(mesh):
    placed = (
        P(None, AXES),
        P(None, AXES),
        P(AXES),
        P(AXES, None, None),
        P(AXES, None, None),
        P(AXES, None, None),
        P(AXES, None, None),
        P(AXES, None),
        P(AXES, None),
        P(AXES, None),
        P(AXES, None),
        P(AXES, None),
        P(AXES, None),
    )
    return jax.shard_map(
        on_device, mesh=mesh, in_specs=placed, out_specs=P(None, AXES), check_vma=False
    )
```
